32 devices in a mesh: grp: 2 (over x), chan: 16 (over z, y, core).
Axes of the slice: x: 2, y: 2, z: 4, core: 2. Of those that a mesh axis runs over, the one named last changes fastest.
Arguments:
- spectra: bfloat16 [128, 4, 2, 4096], P(('grp', 'chan')), parts along dimension 0, may hold values from -60 to 60
- valid: int32 [128, 4], P(('grp', 'chan')), parts along dimension 0, may hold values 0 or 1
- partner: int32 [16], replicated, may hold values from 0 to 15, as said below
- pair_bin: int32 [1024], P(('grp', 'chan')), parts along dimension 0, may hold values from -1 to 127, as said below
- pair_count: int32 [32], P(('grp', 'chan')), parts along dimension 0, may hold values from 24 to 32
Outputs:
- stacked: float32 [256, 1024], P(('grp', 'chan')), parts along dimension 0
The draws below stay inside these ranges and needn't reach their ends.
There are 2 independent parts, one for each index of `grp`. The reference program is written for one: setup_inputs(seed, part) draws one part's arguments, and reference() takes and returns one part's arrays. A program takes and returns all parts, laid end to end along the dimension named above; an argument that names none is the same for every part. Nothing has to cross between parts.
Inputs may be any that keep to these rules, and one draw needn't show every extreme that they name: partner[p] = p XOR r for one r of 1 to 15, the same for every p. `pair_bin`: -1 marks a row without bin, and every row pairing a channel with itself is -1; bin k is owned by block k // 8.
All inputs are finite; a program needn't handle non-finite values. No bound on the sum of `valid` on one device may be relied on, other than what follows from the above.
Results may differ from the reference program's by a relative error of at most 0.0056.
Values may be sent and summed in bfloat16 or wider, within the bound.
No kernel may reach another device: no remote copies, remote signals or barrier semaphores. Data moves between devices by JAX's collectives and lax.ppermute only.
A program may use at most 128 MiB of HBM per device.

```python
import math
import jax
import jax.numpy as jnp
from jax import lax

CH_DEV = 4
WIN = 4
F = 4096
BAND = 128
LAGS = 1024
BINS_DEV = 8
PAIRS_DEV = 32
CHANNELS = 64
BINS = 128
N_CHAN = 16


def draw_spectra(key, part):
    nchan = CH_DEV * N_CHAN
    key_base, key_level = jax.random.split(key)
    shape = (nchan, WIN, 2, F // BAND, BAND)
    base = jnp.clip(jax.random.normal(key_base, shape, jnp.float32), -6.0, 6.0)
    levels = jax.random.uniform(key_level, (nchan, WIN, 1, F // BAND, 1), jnp.float32, 0.0, math.log(10.0))
    values = base * jnp.exp(levels)
    return values.reshape(nchan, WIN, 2, F).astype(jnp.bfloat16)


def draw_partner(key, part):
    offset = jax.random.randint(key, (), 1, N_CHAN, dtype=jnp.int32)
    return jnp.bitwise_xor(jnp.arange(N_CHAN, dtype=jnp.int32), offset)


def draw_pair_bin(key, part):
    total = PAIRS_DEV * N_CHAN
    index = jnp.arange(total, dtype=jnp.int32)
    block = index // PAIRS_DEV
    within = index % PAIRS_DEV
    square = CH_DEV * CH_DEV
    first = within % square // CH_DEV
    second = within % CH_DEV
    itself = (within < square) & (first == second)
    key_reach, key_slot = jax.random.split(key)
    distance = jax.random.randint(key_reach, (total,), 0, N_CHAN, dtype=jnp.int32)
    distance = jnp.where(within == 1, N_CHAN - 1, distance)
    distance = jnp.where(within == 2, N_CHAN // 2, distance)
    slot = jax.random.randint(key_slot, (total,), 0, BINS_DEV, dtype=jnp.int32)
    bins = (block + distance) % N_CHAN * BINS_DEV + slot
    return jnp.where(itself, -1, bins).astype(jnp.int32)


def draw_pair_count(key, part):
    lowest = PAIRS_DEV * 3 // 4
    key_count, key_high, key_step = jax.random.split(key, 3)
    counts = jax.random.randint(key_count, (N_CHAN,), lowest, PAIRS_DEV + 1, dtype=jnp.int32)
    high_at = jax.random.randint(key_high, (), 0, N_CHAN, dtype=jnp.int32)
    low_at = (high_at + jax.random.randint(key_step, (), 1, N_CHAN, dtype=jnp.int32)) % N_CHAN
    index = jnp.arange(N_CHAN, dtype=jnp.int32)
    counts = jnp.where(index == high_at, PAIRS_DEV, counts)
    counts = jnp.where(index == low_at, lowest, counts)
    return counts.astype(jnp.int32)


def set_ends(result, key, smallest, largest):
    dims = result.shape
    spot = [jax.random.randint(jax.random.fold_in(key, axis), (), 0, dims[axis]) for axis in range(len(dims))]
    result = result.at[tuple(spot)].set(smallest)
    longest = dims.index(max(dims))
    spot[longest] = (spot[longest] + 1) % dims[longest]
    return result.at[tuple(spot)].set(largest)


def setup_inputs(seed: int = 0, part: int = 0) -> dict:
    seeds = jax.random.split(jax.random.key(seed), 6)
    part_splits = jax.random.split(jax.random.fold_in(seeds[5], part), 6)
    return {
        "spectra": draw_spectra(jax.random.fold_in(jax.random.fold_in(seeds[5], part), 71), part),
        "valid": set_ends((jax.random.randint(part_splits[1], (CHANNELS, WIN), 0, 4) < 3).astype(jnp.int32), jax.random.fold_in(part_splits[1], 1), 0, 1),
        "partner": draw_partner(jax.random.fold_in(seeds[5], 71), part),
        "pair_bin": draw_pair_bin(jax.random.fold_in(jax.random.fold_in(seeds[5], part), 71), part),
        "pair_count": draw_pair_count(jax.random.fold_in(jax.random.fold_in(seeds[5], part), 71), part),
    }


def whiten(spectra, valid):
    values = spectra.astype(jnp.float32)
    power = values[:, :, 0] * values[:, :, 0] + values[:, :, 1] * values[:, :, 1]
    nchan, nwin, nfreq = power.shape
    banded = lax.optimization_barrier(jnp.mean(power.reshape(nchan, nwin, nfreq // BAND, BAND), axis=-1))
    amplitude = jnp.repeat(jnp.sqrt(banded + 1e-06), BAND, axis=-1)
    weights = valid.astype(jnp.float32)[:, :, None, None]
    return (values * weights / amplitude[:, :, None, :]).astype(jnp.bfloat16)

def lag_table():
    freqs = jnp.arange(F, dtype=jnp.int32)
    shifts = jnp.arange(LAGS, dtype=jnp.int32) - LAGS // 2
    phase = jnp.mod(freqs[:, None] * shifts[None, :], 2 * F)
    angle = phase.astype(jnp.float32) * (2.0 * math.pi / (2 * F))
    scale = 1.0 / math.sqrt(F)
    return jnp.concatenate([jnp.cos(angle) * scale, -jnp.sin(angle) * scale], axis=0).astype(jnp.bfloat16)

def correlate(own_block, other_block, table):
    own_real = own_block[:, :, 0].astype(jnp.float32)
    own_imag = own_block[:, :, 1].astype(jnp.float32)
    oth_real = other_block[:, :, 0].astype(jnp.float32)
    oth_imag = other_block[:, :, 1].astype(jnp.float32)
    real_part = jnp.einsum('awf,bwf->abf', own_real, oth_real) + jnp.einsum('awf,bwf->abf', own_imag, oth_imag)
    imag_part = jnp.einsum('awf,bwf->abf', own_imag, oth_real) - jnp.einsum('awf,bwf->abf', own_real, oth_imag)
    nchan = own_block.shape[0]
    nwin = own_block.shape[1]
    spec = (jnp.concatenate([real_part, imag_part], axis=-1) * (1.0 / nwin)).reshape(nchan * nchan, -1)
    spec = spec.astype(jnp.bfloat16)
    return jnp.dot(spec, table, preferred_element_type=jnp.float32)

def reference(spectra, valid, partner, pair_bin, pair_count):
    white = whiten(spectra, valid)
    blocks = white.reshape(N_CHAN, CH_DEV, WIN, 2, F)
    table = lag_table()

    def one_block(block_index):
        own_block = lax.dynamic_index_in_dim(blocks, block_index, 0, keepdims=False)
        other_index = lax.dynamic_index_in_dim(partner, block_index, 0, keepdims=False)
        other_block = lax.dynamic_index_in_dim(blocks, other_index, 0, keepdims=False)
        return jnp.concatenate([correlate(own_block, own_block, table), correlate(own_block, other_block, table)], axis=0)
    corr_all = lax.map(one_block, jnp.arange(N_CHAN, dtype=jnp.int32))
    bins = pair_bin.reshape(N_CHAN, PAIRS_DEV)
    rows = jnp.arange(PAIRS_DEV, dtype=jnp.int32)
    keep = (rows[None, :] < pair_count[:, None]) & (bins >= 0)
    segment = jnp.where(keep, bins, BINS).reshape(-1)
    summed = jax.ops.segment_sum(corr_all.reshape(-1, LAGS), segment, num_segments=BINS + 1)[:BINS]
    return summed * (1.0 / math.sqrt(PAIRS_DEV // BINS_DEV))
```

```python
import functools
import math

import jax
import jax.numpy as jnp
import numpy as np
from jax import lax
from jax.experimental import pallas as pl
from jax.experimental.pallas import tpu as pltpu
from jax.sharding import PartitionSpec as P

BAND = 128
LAGS = 1024
BINS_DEV = 8
PAIRS_DEV = 32


def transform_tables(nbands):
    nfreq = nbands * BAND
    nm = 2 * nbands
    nq = LAGS // nm
    m = np.arange(nm)
    first = 2.0 * np.pi * ((m[:, None] * np.arange(nbands)[None, :]) % nm) / nm
    cos, sin = np.cos(first), np.sin(first)
    rows = ((cos, -sin), (sin, cos), (cos, sin), (sin, -cos))
    whole = np.concatenate([np.concatenate(row, axis=1) for row in rows], axis=0)
    half = nbands // 2
    halves = np.stack(
        [
            np.concatenate([np.concatenate([part[:, k : k + half] for part in row], axis=1) for row in rows], axis=0)
            for k in (0, half)
        ]
    )
    scale = 1.0 / math.sqrt(nfreq) / math.sqrt(PAIRS_DEV // BINS_DEV)
    angle = 2.0 * np.pi * (m[:, None] * np.arange(BAND)[None, :]) / (2 * nfreq)
    twiddle = np.stack([np.cos(angle), np.sin(angle)]) * scale
    order = np.concatenate([np.arange(0, nq, 2), np.arange(1, nq, 2)]) - nq // 2
    last = 2.0 * np.pi * ((order[:, None] * np.arange(BAND)[None, :]) % BAND) / BAND
    final = np.concatenate([np.cos(last), -np.sin(last)], axis=1)
    return (
        jnp.asarray(whole, jnp.bfloat16),
        jnp.asarray(halves, jnp.bfloat16),
        jnp.asarray(twiddle, jnp.float32),
        jnp.asarray(final, jnp.bfloat16),
    )


def reversed_bits(value, bits):
    return sum((value >> k & 1) << bits - 1 - k for k in range(bits))


def stack_kernel(
    nblocks,
    nchan,
    nwin,
    own_ref,
    oth_ref,
    valid_ref,
    partner_ref,
    own_bins_ref,
    oth_bins_ref,
    whole_ref,
    halves_ref,
    twiddle_ref,
    final_ref,
    keep_ref,
    send_ref,
    split,
    own_white,
    oth_white,
    self_spec,
    cross_spec,
    turned,
    sums,
):
    me = lax.axis_index("chan")
    other = me ^ partner_ref[0]
    upper = (other < me).astype(jnp.int32)
    nbands = own_white.shape[1]
    half = nbands // 2
    nm = 2 * nbands
    trash = nblocks * BINS_DEV

    def white_of(ref, at, bands, weight):
        split[pl.ds(0, 2 * bands), :] = ref[at].astype(jnp.float32)
        real = split[pl.ds(0, bands, stride=2), :]
        imag = split[pl.ds(1, bands, stride=2), :]
        mean = jnp.sum(real * real + imag * imag, axis=-1, keepdims=True) * (1.0 / BAND)
        gain = lax.rsqrt(mean + 1e-06)
        if weight is not None:
            gain = gain * weight
        return [(part * gain).astype(jnp.bfloat16).astype(jnp.float32) for part in (real, imag)]

    for index in range(nblocks * BINS_DEV):
        sums[index] = jnp.zeros(sums.shape[1:], jnp.float32)

    for c in range(nchan):
        for w in range(nwin):
            at = c * nwin + w
            own = white_of(own_ref, at, nbands, valid_ref[c, w].astype(jnp.float32))
            oth = white_of(oth_ref, at, half, None)
            for i in range(2):
                own_white[2 * at + i] = own[i]
                oth_white[2 * at + i] = oth[i]

    def spec_of(left, right):
        real = imag = 0.0
        for w in range(nwin):
            left_real, left_imag = left(w, 0), left(w, 1)
            right_real, right_imag = right(w, 0), right(w, 1)
            real += left_real * right_real + left_imag * right_imag
            imag += left_imag * right_real - left_real * right_imag
        return [(part * (1.0 / nwin)).astype(jnp.bfloat16) for part in (real, imag)]

    own_half = pl.ds(pl.multiple_of(upper * half, half), half)
    self_pairs = [(a, b) for a in range(nchan) for b in range(a + 1, nchan)]
    cross_pairs = [(a, b) for a in range(nchan) for b in range(nchan)]
    for at, (a, b) in enumerate(self_pairs):
        real, imag = spec_of(
            lambda w, i: own_white[2 * (a * nwin + w) + i],
            lambda w, i: own_white[2 * (b * nwin + w) + i],
        )
        self_spec[0:nbands, at * BAND : (at + 1) * BAND] = real
        self_spec[nbands:nm, at * BAND : (at + 1) * BAND] = imag
    for at, (a, b) in enumerate(cross_pairs):
        real, imag = spec_of(
            lambda w, i: own_white[2 * (a * nwin + w) + i, own_half, :],
            lambda w, i: oth_white[2 * (b * nwin + w) + i],
        )
        cross_spec[0:half, at * BAND : (at + 1) * BAND] = real
        cross_spec[half:nbands, at * BAND : (at + 1) * BAND] = imag

    lane = lax.broadcasted_iota(jnp.int32, sums.shape[1:], 1)
    low = lane < nm
    cos, sin = twiddle_ref[0], twiddle_ref[1]

    def add_rows(table, spec, at, targets):
        out = jnp.dot(table, spec[:, at * BAND : (at + 2) * BAND], preferred_element_type=jnp.float32)
        base = 0
        for pair in range(2):
            for way in range(2):
                real = out[2 * way * nm : (2 * way + 1) * nm, pair * BAND : (pair + 1) * BAND]
                imag = out[(2 * way + 1) * nm : (2 * way + 2) * nm, pair * BAND : (pair + 1) * BAND]
                turned[base : base + nm, 0:BAND] = (real * cos - imag * sin).astype(jnp.bfloat16)
                turned[base : base + nm, BAND : 2 * BAND] = (real * sin + imag * cos).astype(jnp.bfloat16)
                base += nm
        corr = lax.dot_general(
            final_ref[...], turned[...], (((1,), (1,)), ((), ())), preferred_element_type=jnp.float32
        )
        nq = corr.shape[0] // 2
        for pair in range(2):
            even = corr[0:nq, pair * BAND : (pair + 1) * BAND]
            odd = corr[nq:, pair * BAND : (pair + 1) * BAND]
            first = jnp.where(low, even, pltpu.roll(odd, nm, 1))
            second = jnp.where(low, pltpu.roll(even, nm, 1), odd)
            for row, (ref, number) in zip((first, second), targets[pair]):
                bin_number = ref[number]
                slot = jnp.where(bin_number >= 0, bin_number ^ (me * BINS_DEV), trash)
                sums[slot] = sums[slot] + row

    for at in range(0, len(self_pairs), 2):
        targets = [
            ((own_bins_ref, a * nchan + b), (own_bins_ref, b * nchan + a)) for a, b in self_pairs[at : at + 2]
        ]
        add_rows(whole_ref[...], self_spec, at, targets)
    square = nchan * nchan
    for at in range(0, len(cross_pairs), 2):
        targets = [
            ((own_bins_ref, square + a * nchan + b), (oth_bins_ref, square + b * nchan + a))
            for a, b in cross_pairs[at : at + 2]
        ]
        add_rows(halves_ref[upper], cross_spec, at, targets)

    bits = nblocks.bit_length() - 1
    rows = BINS_DEV * sums.shape[1]
    for index in range(nblocks):
        block = reversed_bits(index, bits)
        values = sums[block * BINS_DEV : (block + 1) * BINS_DEV].reshape(rows, BAND)
        if index < nblocks // 2:
            keep_ref[index * rows : (index + 1) * rows, :] = values
        else:
            start = (index - nblocks // 2) * rows
            send_ref[start : start + rows, :] = values.astype(jnp.bfloat16)


def swap(values, axis, mask):
    return lax.ppermute(values, axis, [(p, p ^ mask) for p in range(lax.axis_size(axis))])


def on_device(spectra, valid, partner, pair_bin, pair_count):
    nblocks = lax.axis_size("chan")
    nchan, nwin, _, nfreq = spectra.shape
    nbands = nfreq // BAND
    half = nbands // 2
    view = (
        spectra.reshape(nchan * nwin, 2, nbands, BAND)
        .transpose(0, 2, 1, 3)
        .reshape(nchan * nwin, 2 * nbands, BAND)
    )
    usable = valid.astype(jnp.bfloat16).reshape(nchan * nwin, 1, 1)
    rows = jnp.arange(pair_bin.shape[0], dtype=jnp.int32)
    own_bins = jnp.where((rows < pair_count[0]) & (pair_bin >= 0), pair_bin, -1)
    me = lax.axis_index("chan")

    def exchange(mask, view, usable, own_bins):
        lower = 1 - (me >> mask.bit_length() - 1 & 1)
        part = lax.dynamic_slice_in_dim(view, lower * 2 * half, 2 * half, axis=1) * usable
        return swap(part, "chan", mask), swap(own_bins, "chan", mask)

    branches = [functools.partial(exchange, mask) for mask in range(1, nblocks)]
    oth, oth_bins = lax.switch(partner[0] - 1, branches, view, usable, own_bins)

    whole, halves, twiddle, final = transform_tables(nbands)
    nq = LAGS // (2 * nbands)
    npairs = nchan * (nchan - 1) // 2
    rows_out = nblocks // 2 * BINS_DEV * nq // 2
    vmem = pl.BlockSpec(memory_space=pltpu.VMEM)
    smem = pl.BlockSpec(memory_space=pltpu.SMEM)
    keep, send = pl.pallas_call(
        functools.partial(stack_kernel, nblocks, nchan, nwin),
        out_shape=[
            jax.ShapeDtypeStruct((rows_out, BAND), jnp.float32),
            jax.ShapeDtypeStruct((rows_out, BAND), jnp.bfloat16),
        ],
        in_specs=[vmem, vmem, smem, smem, smem, smem, vmem, vmem, vmem, vmem],
        out_specs=[vmem, vmem],
        scratch_shapes=[
            pltpu.VMEM((2 * nbands, BAND), jnp.float32),
            pltpu.VMEM((2 * nchan * nwin, nbands, BAND), jnp.float32),
            pltpu.VMEM((2 * nchan * nwin, half, BAND), jnp.float32),
            pltpu.VMEM((2 * nbands, npairs * BAND), jnp.bfloat16),
            pltpu.VMEM((nbands, nchan * nchan * BAND), jnp.bfloat16),
            pltpu.VMEM((8 * nbands, 2 * BAND), jnp.bfloat16),
            pltpu.VMEM((nblocks * BINS_DEV + 1, nq // 2, BAND), jnp.float32),
        ],
        compiler_params=pltpu.CompilerParams(vmem_limit_bytes=32 * 1024 * 1024),
    )(view, oth, valid, partner, own_bins, oth_bins, whole, halves, twiddle, final)

    sums = keep + swap(send, "chan", 1).astype(jnp.float32)
    mask = 2
    while mask < nblocks:
        count = sums.shape[0] // 2
        received = swap(sums[count:].astype(jnp.bfloat16), "chan", mask)
        sums = sums[:count] + received.astype(jnp.float32)
        mask *= 2
    return sums.reshape(BINS_DEV, LAGS)


def solution(mesh):
    in_specs = (
        P(("grp", "chan"), None, None, None),
        P(("grp", "chan"), None),
        P(),
        P(("grp", "chan")),
        P(("grp", "chan")),
    )
    out_specs = P(("grp", "chan"), None)
    return jax.shard_map(
        on_device, mesh=mesh, in_specs=in_specs, out_specs=out_specs, check_vma=False
    )
```

```python
import functools
import math

import jax
import jax.numpy as jnp
import numpy as np
from jax import lax
from jax.experimental import pallas as pl
from jax.experimental.pallas import tpu as pltpu
from jax.sharding import PartitionSpec as P

BAND = 128
LAGS = 1024
BINS_DEV = 8
PAIRS_DEV = 32


def transform_tables(nbands):
    nfreq = nbands * BAND
    nm = 2 * nbands
    nq = LAGS // nm
    m = np.arange(nm)
    first = 2.0 * np.pi * ((m[:, None] * np.arange(nbands)[None, :]) % nm) / nm
    cos, sin = np.cos(first), np.sin(first)
    rows = ((cos, -sin), (sin, cos))

    def columns(start, stop):
        return np.concatenate([np.concatenate([part[:, start:stop] for part in row], axis=1) for row in rows], axis=0)

    half = nbands // 2
    scale = 1.0 / math.sqrt(nfreq) / math.sqrt(PAIRS_DEV // BINS_DEV)
    angle = 2.0 * np.pi * (m[:, None] * np.arange(BAND)[None, :]) / (2 * nfreq)
    twiddle = np.stack([np.cos(angle), np.sin(angle)]) * scale
    order = np.concatenate([np.arange(0, nq, 2), np.arange(1, nq, 2), np.full(nq // 2, nq)]) - nq // 2
    last = 2.0 * np.pi * ((order[:, None] * np.arange(BAND)[None, :]) % BAND) / BAND
    final = np.concatenate([np.cos(last), -np.sin(last)], axis=1)
    return (
        jnp.asarray(columns(0, nbands), jnp.bfloat16),
        jnp.asarray(np.stack([columns(0, half), columns(half, nbands)]), jnp.bfloat16),
        jnp.asarray(twiddle, jnp.float32),
        jnp.asarray(final, jnp.bfloat16),
    )


def self_pairs(nchan):
    return [(a, b) for a in range(nchan) for b in range(a + 1, nchan)]


def order_tables(nchan):
    reverse = np.zeros((2 * BAND, BAND))
    lane = np.arange(1, BAND)
    reverse[BAND - lane, lane] = 1
    reverse[BAND, 0] = 1
    square = nchan * nchan
    pairs = np.zeros((4 * square, 4 * square))
    for line, (a, b) in enumerate(self_pairs(nchan)):
        pairs[a * nchan + b, line] = 1
        pairs[b * nchan + a, 2 * square + line] = 1
    for a in range(nchan):
        for b in range(nchan):
            line = square + a * nchan + b
            pairs[line, line] = 1
            pairs[3 * square + b * nchan + a, 2 * square + line] = 1
    return jnp.asarray(reverse, jnp.bfloat16), jnp.asarray(pairs, jnp.bfloat16)


def prepare_kernel(raw_hbm, valid_hbm, bins_hbm, count_hbm, raw_ref, valid, bins, count, sems):
    nchan, nwin = valid.shape
    windows, rows = raw_hbm.shape[0], raw_ref.shape[2]
    moves = [(bins_hbm, bins), (count_hbm, count), (valid_hbm, valid)]
    moves += [(raw_hbm.at[:, h * rows : (h + 1) * rows, :], raw_ref.at[h, 0:windows]) for h in range(2)]
    copies = [pltpu.make_async_copy(source, target, sems.at[k]) for k, (source, target) in enumerate(moves)]
    for copy in copies:
        copy.start()
    for copy in copies[:3]:
        copy.wait()
    number = lax.broadcasted_iota(jnp.int32, bins.shape, 1)
    kept = jnp.where(number < count[0], bins[...], -1)
    fill = jnp.zeros((1, BAND - kept.shape[1]), jnp.int32)
    row = lax.broadcasted_iota(jnp.int32, (rows, BAND), 0)
    notes = jnp.zeros((rows, BAND), jnp.int32)
    for place, values in ((0, kept >> 3), (1, kept & BINS_DEV - 1)):
        notes = jnp.where(row == place, jnp.concatenate([values, fill], axis=1), notes)
    for at in range(windows):
        c, w = at // nwin, at % nwin
        notes = jnp.where(row == rows - windows + at, valid[c, w], notes)
    for h in range(2):
        raw_ref[h, windows] = notes.astype(jnp.float32).astype(jnp.bfloat16)
    for copy in copies[3:]:
        copy.wait()


def bins_of(notes, count):
    digits = notes.astype(jnp.float32).astype(jnp.int32)
    return digits[0:1, 0:count] * BINS_DEV + digits[1:2, 0:count]


def valid_of(notes, windows, at):
    row = notes.shape[0] - windows + at
    return notes[row : row + 1, :]


def whiten(raw, valid, split):
    split[...] = raw.astype(jnp.float32)
    bands = split.shape[0] // 2
    real = split[pl.ds(0, bands, stride=2), :]
    imag = split[pl.ds(1, bands, stride=2), :]
    mean = jnp.sum(real * real + imag * imag, axis=-1, keepdims=True) * (1.0 / BAND)
    gain = lax.rsqrt(mean + 1e-06) * valid
    return [(part * gain).astype(jnp.bfloat16) for part in (real, imag)]


def cross_spectrum(left, right):
    real = imag = 0.0
    for (left_real, left_imag), (right_real, right_imag) in zip(left, right):
        real += left_real * right_real + left_imag * right_imag
        imag += left_imag * right_real - left_real * right_imag
    return [(part * (1.0 / len(left))).astype(jnp.bfloat16) for part in (real, imag)]


def lag_lines(table, spec, twiddle_ref, final, turned, numbers, lines, stride):
    nm = twiddle_ref.shape[1]
    cos, sin = twiddle_ref[0], twiddle_ref[1]
    out = jnp.dot(table, spec, preferred_element_type=jnp.float32)
    for at in range(len(numbers)):
        real = out[:nm, at * BAND : (at + 1) * BAND]
        imag = out[nm:, at * BAND : (at + 1) * BAND]
        turned[at * nm : (at + 1) * nm, 0:BAND] = (real * cos - imag * sin).astype(jnp.bfloat16)
        turned[at * nm : (at + 1) * nm, BAND : 2 * BAND] = (real * sin + imag * cos).astype(jnp.bfloat16)
    corr = lax.dot_general(final, turned[...], (((1,), (1,)), ((), ())), preferred_element_type=jnp.float32)
    nq = corr.shape[0] // 3
    low = lax.broadcasted_iota(jnp.int32, (nq, BAND), 1) < nm
    for at in range(0, len(numbers), 2):
        even, odd, beyond = (corr[k * nq : (k + 1) * nq, at * nm : (at + 2) * nm] for k in range(3))
        lines[pl.ds(numbers[at], nq, stride=stride), :] = jnp.where(low, even, pltpu.roll(odd, nm, 1))
        lines[pl.ds(numbers[at + 1], nq, stride=stride), :] = jnp.where(low, pltpu.roll(even, nm, 1), odd)
        for k in range(2):
            row = nq * stride + numbers[at + k]
            lines[row : row + 1, :] = (pltpu.roll(beyond, nm, 1) if k else beyond)[0:1, :]


def self_kernel(raw_ref, table_ref, twiddle_ref, final_ref, white_ref, lines_ref, split, spec, turned, *, nchan, nwin):
    half = white_ref.shape[2]
    lines_ref[...] = jnp.zeros(lines_ref.shape, jnp.float32)
    notes = raw_ref[0, nchan * nwin].astype(jnp.float32)
    for h in range(2):
        for at in range(nchan * nwin):
            valid = valid_of(notes, nchan * nwin, at)
            white = whiten(raw_ref[h, at], valid, split.at[h * nchan * nwin + at])
            for i in range(2):
                white_ref[h, 2 * at + i] = white[i]
        channels = [
            [[white_ref[h, 2 * (c * nwin + w) + i].astype(jnp.float32) for i in range(2)] for w in range(nwin)]
            for c in range(nchan)
        ]
        for at, (a, b) in enumerate(self_pairs(nchan)):
            real, imag = cross_spectrum(channels[a], channels[b])
            spec[h * half : (h + 1) * half, at * BAND : (at + 1) * BAND] = real
            spec[(2 + h) * half : (3 + h) * half, at * BAND : (at + 1) * BAND] = imag
    numbers = range(len(self_pairs(nchan)))
    lag_lines(table_ref[...], spec[...], twiddle_ref, final_ref[...], turned, numbers, lines_ref, nchan * nchan)


def reversed_bits(value, bits):
    return sum((value >> k & 1) << bits - 1 - k for k in range(bits))


def stack_kernel(
    part_ref,
    white_ref,
    self_ref,
    own_notes_ref,
    table_ref,
    twiddle_ref,
    final_ref,
    reverse_ref,
    pairs_ref,
    keep_ref,
    send_ref,
    split,
    spec,
    turned,
    lines,
    *,
    nblocks,
    nchan,
    nwin,
):
    me = lax.axis_index("chan")
    half = white_ref.shape[1]
    square = nchan * nchan
    nq = lines.shape[0] // (2 * square) - 1
    for q in range(nq + 1):
        lines[q * 2 * square : q * 2 * square + square, :] = self_ref[q * square : (q + 1) * square, :]
        if q == nq:
            start = q * 2 * square + square
            lines[start : start + square, :] = jnp.zeros((square, BAND), jnp.float32)
    others = []
    notes = part_ref[nchan * nwin].astype(jnp.float32)
    for b in range(nchan):
        windows = [
            whiten(part_ref[at], valid_of(notes, nchan * nwin, at), split.at[at])
            for at in range(b * nwin, (b + 1) * nwin)
        ]
        others.append([[part.astype(jnp.float32) for part in parts] for parts in windows])
    for a in range(nchan):
        own = [[white_ref[2 * (a * nwin + w) + i].astype(jnp.float32) for i in range(2)] for w in range(nwin)]
        for b in range(nchan):
            real, imag = cross_spectrum(own, others[b])
            spec[a, 0:half, b * BAND : (b + 1) * BAND] = real
            spec[a, half : 2 * half, b * BAND : (b + 1) * BAND] = imag
    for a in range(nchan):
        numbers = [square + a * nchan + b for b in range(nchan)]
        lag_lines(
            table_ref[...], spec[a], twiddle_ref, final_ref[...], turned.at[a], numbers, lines, 2 * square
        )
    forward = [lines[q * 2 * square : (q + 1) * 2 * square, :].astype(jnp.bfloat16) for q in range(nq + 1)]
    pairs = jnp.concatenate(
        [
            jnp.concatenate([forward[nq - 1 - q] for q in range(nq)], axis=0),
            jnp.concatenate([forward[nq - q] for q in range(nq)], axis=0),
        ],
        axis=1,
    )
    backward = jnp.dot(pairs, reverse_ref[...], preferred_element_type=jnp.float32).astype(jnp.bfloat16)
    both = jnp.concatenate(
        [
            jnp.concatenate(forward[:nq], axis=1),
            jnp.concatenate([backward[q * 2 * square : (q + 1) * 2 * square, :] for q in range(nq)], axis=1),
        ],
        axis=0,
    )

    bits = nblocks.bit_length() - 1
    chunk = min(nblocks // 2, 8)
    bins = jnp.concatenate(
        [bins_of(values, 2 * square) for values in (own_notes_ref[...], part_ref[nchan * nwin])], axis=1
    )
    target = jnp.where(bins >= 0, bins ^ (me * BINS_DEV), -1)
    for out_ref, base in ((keep_ref, 0), (send_ref, nblocks // 2)):

        def add(index, _, out_ref=out_ref, base=base):
            place = lax.broadcasted_iota(jnp.int32, (chunk * BINS_DEV, 4 * square), 0) + (
                (base + index * chunk) * BINS_DEV
            )
            owned = (reversed_bits(place >> 3, bits) << 3) + (place & BINS_DEV - 1)
            chosen = (owned == target).astype(jnp.float32).astype(jnp.bfloat16)
            chosen = jnp.dot(chosen, pairs_ref[...], preferred_element_type=jnp.float32).astype(jnp.bfloat16)
            sums = jnp.dot(chosen, both, preferred_element_type=jnp.float32)
            for block in range(chunk):
                for q in range(0, nq, 2):
                    tile = jnp.concatenate(
                        [
                            sums[block * BINS_DEV : (block + 1) * BINS_DEV, k * BAND : (k + 1) * BAND]
                            for k in (q, q + 1)
                        ],
                        axis=0,
                    )
                    start = (index * chunk + block) * nq * BINS_DEV + q * BINS_DEV
                    if not isinstance(start, int):
                        start = pl.multiple_of(start, 2 * BINS_DEV)
                    out_ref[pl.ds(start, 2 * BINS_DEV), :] = tile.astype(out_ref.dtype)

        count = nblocks // 2 // chunk
        if count == 1:
            add(0, None)
        else:
            lax.fori_loop(0, count, add, None)


def swap(values, axis, mask):
    return lax.ppermute(values, axis, [(p, p ^ mask) for p in range(lax.axis_size(axis))])


def on_device(spectra, valid, partner, pair_bin, pair_count):
    nblocks = lax.axis_size("chan")
    nchan, nwin, _, nfreq = spectra.shape
    nbands = nfreq // BAND
    half = nbands // 2
    nm = 2 * nbands
    nq = LAGS // nm // 2
    square = nchan * nchan
    windows = nchan * nwin
    npairs = len(self_pairs(nchan))
    me = lax.axis_index("chan")
    raw = spectra.reshape(windows, 2, nbands, BAND).transpose(0, 2, 1, 3).reshape(windows, 2 * nbands, BAND)
    whole, halves, twiddle, final = transform_tables(nbands)
    reverse, pairs = order_tables(nchan)
    vmem = pl.BlockSpec(memory_space=pltpu.VMEM)
    hbm = pl.BlockSpec(memory_space=pltpu.HBM)
    params = pltpu.CompilerParams(vmem_limit_bytes=32 * 1024 * 1024)

    raw = pl.pallas_call(
        prepare_kernel,
        out_shape=jax.ShapeDtypeStruct((2, windows + 1, nbands, BAND), jnp.bfloat16),
        in_specs=[hbm] * 4,
        out_specs=vmem,
        scratch_shapes=[
            pltpu.SMEM(valid.shape, jnp.int32),
            pltpu.VMEM((1, pair_bin.shape[0]), jnp.int32),
            pltpu.SMEM((1,), jnp.int32),
            pltpu.SemaphoreType.DMA((5,)),
        ],
    )(raw, valid, pair_bin.reshape(1, -1), pair_count)

    def own_lines(raw, upper):
        white, lines = pl.pallas_call(
            functools.partial(self_kernel, nchan=nchan, nwin=nwin),
            out_shape=[
                jax.ShapeDtypeStruct((2, 2 * windows, half, BAND), jnp.bfloat16),
                jax.ShapeDtypeStruct(((nq + 1) * square, BAND), jnp.float32),
            ],
            in_specs=[vmem] * 4,
            out_specs=[vmem] * 2,
            scratch_shapes=[
                pltpu.VMEM((2 * windows, nbands, BAND), jnp.float32),
                pltpu.VMEM((nm, npairs * BAND), jnp.bfloat16),
                pltpu.VMEM((npairs * nm, 2 * BAND), jnp.bfloat16),
            ],
            compiler_params=params,
        )(raw, whole, twiddle, final)
        table = lax.dynamic_index_in_dim(halves, upper, 0, keepdims=False)
        return lax.dynamic_index_in_dim(white, upper, 0, keepdims=False), lines, table

    def branch(mask, raw):
        upper = me >> mask.bit_length() - 1 & 1
        part = lax.dynamic_index_in_dim(raw, 1 - upper, 0, keepdims=False)
        return swap(part, "chan", mask), *own_lines(raw, upper)

    round_mask = partner[0]
    if nblocks <= 16:
        branches = [functools.partial(branch, mask) for mask in range(1, nblocks)]
        part, white, lines, table = lax.switch(round_mask - 1, branches, raw)
    else:
        upper = (me ^ round_mask < me).astype(jnp.int32)
        part = lax.dynamic_index_in_dim(raw, 1 - upper, 0, keepdims=False)
        for bit in range(nblocks.bit_length() - 1):
            part = jnp.where(round_mask >> bit & 1 == 1, swap(part, "chan", 1 << bit), part)
        white, lines, table = own_lines(raw, upper)

    rows = nblocks // 2 * BINS_DEV * nq
    keep, send = pl.pallas_call(
        functools.partial(stack_kernel, nblocks=nblocks, nchan=nchan, nwin=nwin),
        out_shape=[
            jax.ShapeDtypeStruct((rows, BAND), jnp.float32),
            jax.ShapeDtypeStruct((rows, BAND), jnp.bfloat16),
        ],
        in_specs=[vmem] * 9,
        out_specs=[vmem] * 2,
        scratch_shapes=[
            pltpu.VMEM((windows, nbands, BAND), jnp.float32),
            pltpu.VMEM((nchan, nbands, nchan * BAND), jnp.bfloat16),
            pltpu.VMEM((nchan, nchan * nm, 2 * BAND), jnp.bfloat16),
            pltpu.VMEM(((nq + 1) * 2 * square, BAND), jnp.float32),
        ],
        compiler_params=params,
    )(part, white, lines, raw[0, windows], table, twiddle, final, reverse, pairs)

    sums = keep + swap(send, "chan", 1).astype(jnp.float32)
    mask = 2
    while mask < nblocks:
        rows = sums.shape[0] // 2
        received = swap(sums[rows:].astype(jnp.bfloat16), "chan", mask)
        sums = sums[:rows] + received.astype(jnp.float32)
        mask *= 2
    return sums.reshape(nq, BINS_DEV, BAND).transpose(1, 0, 2).reshape(BINS_DEV, LAGS)


def solution(mesh):
    in_specs = (
        P(("grp", "chan"), None, None, None),
        P(("grp", "chan"), None),
        P(),
        P(("grp", "chan")),
        P(("grp", "chan")),
    )
    out_specs = P(("grp", "chan"), None)
    return jax.shard_map(
        on_device, mesh=mesh, in_specs=in_specs, out_specs=out_specs, check_vma=False
    )
```

```python
import functools
import math

import jax
import jax.numpy as jnp
import numpy as np
from jax import lax
from jax.experimental import pallas as pl
from jax.experimental.pallas import tpu as pltpu
from jax.sharding import PartitionSpec as P

BAND = 128
LAGS = 1024
BINS_DEV = 8
PAIRS_DEV = 32


def self_pairs(nchan):
    return [(a, b) for a in range(nchan) for b in range(a + 1, nchan)]


def tables(nbands, nchan):
    nfreq = nbands * BAND
    half = nbands // 2
    nm = 2 * nbands
    nq = LAGS // nm
    square = nchan * nchan
    m = np.arange(nm)
    first = 2.0 * np.pi * ((m[:, None] * np.arange(nbands)[None, :]) % nm) / nm
    cos, sin = np.cos(first), np.sin(first)
    order = np.concatenate([np.arange(0, nq, 2), np.arange(1, nq, 2), np.full(nq // 2, nq)]) - nq // 2
    last = 2.0 * np.pi * ((order[:, None] * np.arange(BAND)[None, :]) % BAND) / BAND
    basis = np.zeros((2 * nm + 3 * nq // 2, 2 * BAND))
    for h in range(2):
        part = slice(h * half, (h + 1) * half)
        at = h * nbands
        basis[:nm, at : at + nbands] = np.concatenate([cos[:, part], -sin[:, part]], axis=1)
        basis[nm : 2 * nm, at : at + nbands] = np.concatenate([sin[:, part], cos[:, part]], axis=1)
    for line, (a, b) in enumerate(self_pairs(nchan)):
        basis[a * nchan + b, nm + line] = 1
        basis[b * nchan + a, nm + 2 * square + line] = 1
    for a in range(nchan):
        for b in range(nchan):
            line = square + a * nchan + b
            basis[line, nm + line] = 1
            basis[3 * square + b * nchan + a, nm + 2 * square + line] = 1
    lane = np.arange(1, BAND)
    basis[BAND - lane, BAND + lane] = 1
    basis[2 * nm :] = np.concatenate([np.cos(last), -np.sin(last)], axis=1)
    scale = 1.0 / math.sqrt(nfreq) / math.sqrt(PAIRS_DEV // BINS_DEV)
    angle = 2.0 * np.pi * (m[:, None] * np.arange(BAND)[None, :]) / (2 * nfreq)
    twiddle = np.stack([np.cos(angle), np.sin(angle)]) * scale
    return jnp.asarray(basis, jnp.bfloat16), jnp.asarray(twiddle, jnp.float32)


def prepare_kernel(raw_hbm, valid_hbm, bins_hbm, count_hbm, raw_ref, valid, bins, count, sems):
    nchan, nwin = valid.shape
    windows, rows = raw_hbm.shape[0], raw_ref.shape[2]
    moves = [(bins_hbm, bins), (count_hbm, count), (valid_hbm, valid)]
    moves += [(raw_hbm.at[:, h * rows : (h + 1) * rows, :], raw_ref.at[h, 0:windows]) for h in range(2)]
    copies = [pltpu.make_async_copy(source, target, sems.at[k]) for k, (source, target) in enumerate(moves)]
    for copy in copies:
        copy.start()
    for copy in copies[:3]:
        copy.wait()
    number = lax.broadcasted_iota(jnp.int32, bins.shape, 1)
    kept = jnp.where(number < count[0], bins[...], -1)
    fill = jnp.zeros((1, BAND - kept.shape[1]), jnp.int32)
    row = lax.broadcasted_iota(jnp.int32, (rows, BAND), 0)
    notes = jnp.zeros((rows, BAND), jnp.int32)
    for place, values in ((0, kept >> 3), (1, kept & BINS_DEV - 1)):
        notes = jnp.where(row == place, jnp.concatenate([values, fill], axis=1), notes)
    for at in range(windows):
        c, w = at // nwin, at % nwin
        notes = jnp.where(row == rows - windows + at, valid[c, w], notes)
    for h in range(2):
        raw_ref[h, windows] = notes.astype(jnp.float32).astype(jnp.bfloat16)
    for copy in copies[3:]:
        copy.wait()


def bins_of(notes, count):
    digits = notes.astype(jnp.float32).astype(jnp.int32)
    return digits[0:1, 0:count] * BINS_DEV + digits[1:2, 0:count]


def valid_of(notes, windows, at):
    row = notes.shape[0] - windows + at
    return notes[row : row + 1, :]


def whiten(raw, valid, split):
    split[...] = raw.astype(jnp.float32)
    bands = split.shape[0] // 2
    real = split[pl.ds(0, bands, stride=2), :]
    imag = split[pl.ds(1, bands, stride=2), :]
    mean = jnp.sum(real * real + imag * imag, axis=-1, keepdims=True) * (1.0 / BAND)
    gain = lax.rsqrt(mean + 1e-06) * valid
    return [(part * gain).astype(jnp.bfloat16) for part in (real, imag)]


def cross_spectrum(left, right):
    real = imag = 0.0
    for (left_real, left_imag), (right_real, right_imag) in zip(left, right):
        real += left_real * right_real + left_imag * right_imag
        imag += left_imag * right_real - left_real * right_imag
    return [(part * (1.0 / len(left))).astype(jnp.bfloat16) for part in (real, imag)]


def lag_lines(table, spec, twiddle_ref, final, turned, numbers, lines, stride):
    nm = twiddle_ref.shape[1]
    cos, sin = twiddle_ref[0], twiddle_ref[1]
    out = jnp.dot(table, spec, preferred_element_type=jnp.float32)
    for at in range(len(numbers)):
        real = out[:nm, at * BAND : (at + 1) * BAND]
        imag = out[nm:, at * BAND : (at + 1) * BAND]
        turned[at * nm : (at + 1) * nm, 0:BAND] = (real * cos - imag * sin).astype(jnp.bfloat16)
        turned[at * nm : (at + 1) * nm, BAND : 2 * BAND] = (real * sin + imag * cos).astype(jnp.bfloat16)
    corr = lax.dot_general(final, turned[...], (((1,), (1,)), ((), ())), preferred_element_type=jnp.float32)
    nq = corr.shape[0] // 3
    low = lax.broadcasted_iota(jnp.int32, (nq, BAND), 1) < nm
    for at in range(0, len(numbers), 2):
        even, odd, beyond = (corr[k * nq : (k + 1) * nq, at * nm : (at + 2) * nm] for k in range(3))
        lines[pl.ds(numbers[at], nq, stride=stride), :] = jnp.where(low, even, pltpu.roll(odd, nm, 1))
        lines[pl.ds(numbers[at + 1], nq, stride=stride), :] = jnp.where(low, pltpu.roll(even, nm, 1), odd)
        for k in range(2):
            row = nq * stride + numbers[at + k]
            lines[row : row + 1, :] = (pltpu.roll(beyond, nm, 1) if k else beyond)[0:1, :]


def self_kernel(raw_ref, basis_ref, twiddle_ref, white_ref, lines_ref, split, spec, turned, *, nchan, nwin):
    half = white_ref.shape[2]
    lines_ref[...] = jnp.zeros(lines_ref.shape, jnp.float32)
    notes = raw_ref[0, nchan * nwin].astype(jnp.float32)
    for h in range(2):
        for at in range(nchan * nwin):
            valid = valid_of(notes, nchan * nwin, at)
            white = whiten(raw_ref[h, at], valid, split.at[h * nchan * nwin + at])
            for i in range(2):
                white_ref[h, 2 * at + i] = white[i]
        channels = [
            [[white_ref[h, 2 * (c * nwin + w) + i].astype(jnp.float32) for i in range(2)] for w in range(nwin)]
            for c in range(nchan)
        ]
        for at, (a, b) in enumerate(self_pairs(nchan)):
            real, imag = cross_spectrum(channels[a], channels[b])
            spec[2 * h * half : (2 * h + 1) * half, at * BAND : (at + 1) * BAND] = real
            spec[(2 * h + 1) * half : (2 * h + 2) * half, at * BAND : (at + 1) * BAND] = imag
    numbers = range(len(self_pairs(nchan)))
    nm = twiddle_ref.shape[1]
    lag_lines(
        basis_ref[0 : 2 * nm, 0:nm], spec[...], twiddle_ref, basis_ref[2 * nm :, :], turned, numbers, lines_ref, nchan * nchan
    )


def reversed_bits(value, bits):
    return sum((value >> k & 1) << bits - 1 - k for k in range(bits))


def stack_kernel(
    part_ref,
    white_ref,
    self_ref,
    own_notes_ref,
    table_ref,
    basis_ref,
    twiddle_ref,
    keep_ref,
    send_ref,
    split,
    spec,
    turned,
    lines,
    *,
    nblocks,
    nchan,
    nwin,
):
    me = lax.axis_index("chan")
    half = white_ref.shape[1]
    square = nchan * nchan
    nq = lines.shape[0] // (2 * square) - 1
    nm = twiddle_ref.shape[1]
    for q in range(nq + 1):
        lines[q * 2 * square : q * 2 * square + square, :] = self_ref[q * square : (q + 1) * square, :]
        if q == nq:
            start = q * 2 * square + square
            lines[start : start + square, :] = jnp.zeros((square, BAND), jnp.float32)
    others = []
    notes = part_ref[nchan * nwin].astype(jnp.float32)
    for b in range(nchan):
        windows = [
            whiten(part_ref[at], valid_of(notes, nchan * nwin, at), split.at[at])
            for at in range(b * nwin, (b + 1) * nwin)
        ]
        others.append([[part.astype(jnp.float32) for part in parts] for parts in windows])
    for a in range(nchan):
        own = [[white_ref[2 * (a * nwin + w) + i].astype(jnp.float32) for i in range(2)] for w in range(nwin)]
        for b in range(nchan):
            real, imag = cross_spectrum(own, others[b])
            spec[a, 0:half, b * BAND : (b + 1) * BAND] = real
            spec[a, half : 2 * half, b * BAND : (b + 1) * BAND] = imag
    for a in range(nchan):
        numbers = [square + a * nchan + b for b in range(nchan)]
        lag_lines(
            table_ref[...], spec[a], twiddle_ref, basis_ref[2 * nm :, :], turned.at[a], numbers, lines, 2 * square
        )
    exact = [lines[q * 2 * square : (q + 1) * 2 * square, :] for q in range(nq + 1)]
    forward = [block.astype(jnp.bfloat16) for block in exact]
    negated = jnp.dot(
        jnp.concatenate([forward[nq - 1 - q] for q in range(nq)], axis=0),
        basis_ref[0:BAND, BAND : 2 * BAND],
        preferred_element_type=jnp.float32,
    )
    lane = lax.broadcasted_iota(jnp.int32, exact[0].shape, 1)
    backward = [
        jnp.where(lane == 0, exact[nq - q], negated[q * 2 * square : (q + 1) * 2 * square, :]).astype(jnp.bfloat16)
        for q in range(nq)
    ]
    both = jnp.concatenate([jnp.concatenate(parts, axis=1) for parts in (forward[:nq], backward)], axis=0)

    bits = nblocks.bit_length() - 1
    chunk = min(nblocks // 2, 8)
    bins = jnp.concatenate(
        [bins_of(values, 2 * square) for values in (own_notes_ref[...], part_ref[nchan * nwin])], axis=1
    )
    target = jnp.where(bins >= 0, bins ^ (me * BINS_DEV), -1)
    for out_ref, base in ((keep_ref, 0), (send_ref, nblocks // 2)):

        def add(index, _, out_ref=out_ref, base=base):
            place = lax.broadcasted_iota(jnp.int32, (chunk * BINS_DEV, 4 * square), 0) + (
                (base + index * chunk) * BINS_DEV
            )
            owned = (reversed_bits(place >> 3, bits) << 3) + (place & BINS_DEV - 1)
            chosen = (owned == target).astype(jnp.float32).astype(jnp.bfloat16)
            chosen = jnp.dot(chosen, basis_ref[0 : 4 * square, nm : 2 * nm], preferred_element_type=jnp.float32).astype(jnp.bfloat16)
            sums = jnp.dot(chosen, both, preferred_element_type=jnp.float32)
            for block in range(chunk):
                for q in range(0, nq, 2):
                    tile = jnp.concatenate(
                        [
                            sums[block * BINS_DEV : (block + 1) * BINS_DEV, k * BAND : (k + 1) * BAND]
                            for k in (q, q + 1)
                        ],
                        axis=0,
                    )
                    start = (index * chunk + block) * nq * BINS_DEV + q * BINS_DEV
                    if not isinstance(start, int):
                        start = pl.multiple_of(start, 2 * BINS_DEV)
                    out_ref[pl.ds(start, 2 * BINS_DEV), :] = tile.astype(out_ref.dtype)

        count = nblocks // 2 // chunk
        if count == 1:
            add(0, None)
        else:
            lax.fori_loop(0, count, add, None)


def swap(values, axis, mask):
    return lax.ppermute(values, axis, [(p, p ^ mask) for p in range(lax.axis_size(axis))])


def on_device(spectra, valid, partner, pair_bin, pair_count):
    nblocks = lax.axis_size("chan")
    nchan, nwin, _, nfreq = spectra.shape
    nbands = nfreq // BAND
    half = nbands // 2
    nm = 2 * nbands
    nq = LAGS // nm // 2
    square = nchan * nchan
    windows = nchan * nwin
    npairs = len(self_pairs(nchan))
    me = lax.axis_index("chan")
    raw = spectra.reshape(windows, 2, nbands, BAND).transpose(0, 2, 1, 3).reshape(windows, 2 * nbands, BAND)
    basis, twiddle = tables(nbands, nchan)
    vmem = pl.BlockSpec(memory_space=pltpu.VMEM)
    hbm = pl.BlockSpec(memory_space=pltpu.HBM)
    params = pltpu.CompilerParams(vmem_limit_bytes=32 * 1024 * 1024)

    raw = pl.pallas_call(
        prepare_kernel,
        out_shape=jax.ShapeDtypeStruct((2, windows + 1, nbands, BAND), jnp.bfloat16),
        in_specs=[hbm] * 4,
        out_specs=vmem,
        scratch_shapes=[
            pltpu.SMEM(valid.shape, jnp.int32),
            pltpu.VMEM((1, pair_bin.shape[0]), jnp.int32),
            pltpu.SMEM((1,), jnp.int32),
            pltpu.SemaphoreType.DMA((5,)),
        ],
    )(raw, valid, pair_bin.reshape(1, -1), pair_count)

    def own_lines(raw, upper):
        white, lines = pl.pallas_call(
            functools.partial(self_kernel, nchan=nchan, nwin=nwin),
            out_shape=[
                jax.ShapeDtypeStruct((2, 2 * windows, half, BAND), jnp.bfloat16),
                jax.ShapeDtypeStruct(((nq + 1) * square, BAND), jnp.float32),
            ],
            in_specs=[vmem] * 3,
            out_specs=[vmem] * 2,
            scratch_shapes=[
                pltpu.VMEM((2 * windows, nbands, BAND), jnp.float32),
                pltpu.VMEM((nm, npairs * BAND), jnp.bfloat16),
                pltpu.VMEM((npairs * nm, 2 * BAND), jnp.bfloat16),
            ],
            compiler_params=params,
        )(raw, basis, twiddle)
        table = lax.dynamic_slice(basis, (0, upper * nbands), (2 * nm, nbands))
        return lax.dynamic_index_in_dim(white, upper, 0, keepdims=False), lines, table

    def stack(part, white, lines, table, raw):
        rows = nblocks // 2 * BINS_DEV * nq
        keep, send = pl.pallas_call(
            functools.partial(stack_kernel, nblocks=nblocks, nchan=nchan, nwin=nwin),
            out_shape=[
                jax.ShapeDtypeStruct((rows, BAND), jnp.float32),
                jax.ShapeDtypeStruct((rows, BAND), jnp.bfloat16),
            ],
            in_specs=[vmem] * 7,
            out_specs=[vmem] * 2,
            scratch_shapes=[
                pltpu.VMEM((windows, nbands, BAND), jnp.float32),
                pltpu.VMEM((nchan, nbands, nchan * BAND), jnp.bfloat16),
                pltpu.VMEM((nchan, nchan * nm, 2 * BAND), jnp.bfloat16),
                pltpu.VMEM(((nq + 1) * 2 * square, BAND), jnp.float32),
            ],
            compiler_params=params,
        )(part, white, lines, raw[0, windows], table, basis, twiddle)

        return keep, send

    def branch(mask, raw):
        upper = me >> mask.bit_length() - 1 & 1
        part = swap(lax.dynamic_index_in_dim(raw, 1 - upper, 0, keepdims=False), "chan", mask)
        return stack(part, *own_lines(raw, upper), raw)

    round_mask = partner[0]
    if nblocks <= 16:
        branches = [functools.partial(branch, mask) for mask in range(1, nblocks)]
        keep, send = lax.switch(round_mask - 1, branches, raw)
    else:
        upper = ((me ^ round_mask) < me).astype(jnp.int32)
        part = lax.dynamic_index_in_dim(raw, 1 - upper, 0, keepdims=False)
        for bit in range(nblocks.bit_length() - 1):
            part = jnp.where(round_mask >> bit & 1 == 1, swap(part, "chan", 1 << bit), part)
        keep, send = stack(part, *own_lines(raw, upper), raw)

    sums = keep + swap(send, "chan", 1).astype(jnp.float32)
    mask = 2
    while mask < nblocks:
        rows = sums.shape[0] // 2
        received = swap(sums[rows:].astype(jnp.bfloat16), "chan", mask)
        sums = sums[:rows] + received.astype(jnp.float32)
        mask *= 2
    return sums.reshape(nq, BINS_DEV, BAND).transpose(1, 0, 2).reshape(BINS_DEV, LAGS)


def solution(mesh):
    in_specs = (
        P(("grp", "chan"), None, None, None),
        P(("grp", "chan"), None),
        P(),
        P(("grp", "chan")),
        P(("grp", "chan")),
    )
    out_specs = P(("grp", "chan"), None)
    return jax.shard_map(
        on_device, mesh=mesh, in_specs=in_specs, out_specs=out_specs, check_vma=False
    )
```

```python
import functools
import math

import jax
import jax.numpy as jnp
import numpy as np
from jax import lax
from jax.experimental import pallas as pl
from jax.experimental.pallas import tpu as pltpu
from jax.sharding import PartitionSpec as P

BAND = 128
LAGS = 1024
BINS_DEV = 8
PAIRS_DEV = 32


def self_pairs(nchan):
    return [(a, b) for a in range(nchan) for b in range(a + 1, nchan)]


def tables(nbands, nchan):
    nfreq = nbands * BAND
    half = nbands // 2
    nm = 2 * nbands
    nq = LAGS // nm
    square = nchan * nchan
    m = np.arange(nm)
    first = 2.0 * np.pi * ((m[:, None] * np.arange(nbands)[None, :]) % nm) / nm
    cos, sin = np.cos(first), np.sin(first)
    order = np.concatenate([np.arange(0, nq, 2), np.arange(1, nq, 2), np.full(nq // 2, nq)]) - nq // 2
    last = 2.0 * np.pi * ((order[:, None] * np.arange(BAND)[None, :]) % BAND) / BAND
    basis = np.zeros((2 * nm + 3 * nq // 2, 2 * BAND))
    for h in range(2):
        part = slice(h * half, (h + 1) * half)
        at = h * nbands
        basis[:nm, at : at + nbands] = np.concatenate([cos[:, part], -sin[:, part]], axis=1)
        basis[nm : 2 * nm, at : at + nbands] = np.concatenate([sin[:, part], cos[:, part]], axis=1)
    for line, (a, b) in enumerate(self_pairs(nchan)):
        basis[a * nchan + b, nm + line] = 1
        basis[b * nchan + a, nm + 2 * square + line] = 1
    for a in range(nchan):
        for b in range(nchan):
            line = square + a * nchan + b
            basis[line, nm + line] = 1
            basis[3 * square + b * nchan + a, nm + 2 * square + line] = 1
    lane = np.arange(1, BAND)
    basis[BAND - lane, BAND + lane] = 1
    basis[2 * nm :] = np.concatenate([np.cos(last), -np.sin(last)], axis=1)
    scale = 1.0 / math.sqrt(nfreq) / math.sqrt(PAIRS_DEV // BINS_DEV)
    angle = 2.0 * np.pi * (m[:, None] * np.arange(BAND)[None, :]) / (2 * nfreq)
    twiddle = np.stack([np.cos(angle), np.sin(angle)]) * scale
    return jnp.asarray(basis, jnp.bfloat16), jnp.asarray(twiddle, jnp.float32)


def prepare_kernel(
    raw_hbm, valid_hbm, partner_hbm, bins_hbm, count_hbm, raw_ref, own_ref, valid, partner, bins, count, sems
):
    nchan, nwin = valid.shape
    windows, rows = raw_hbm.shape[0], raw_ref.shape[2]
    moves = [(bins_hbm, bins), (count_hbm, count), (valid_hbm, valid), (partner_hbm, partner)]
    moves += [(raw_hbm.at[:, h * rows : (h + 1) * rows, :], raw_ref.at[h, 0:windows]) for h in range(2)]
    copies = [pltpu.make_async_copy(source, target, sems.at[k]) for k, (source, target) in enumerate(moves)]
    for copy in copies:
        copy.start()
    for copy in copies[:4]:
        copy.wait()
    number = lax.broadcasted_iota(jnp.int32, bins.shape, 1)
    kept = jnp.where(number < count[0], bins[...], -1)
    total = kept.shape[1]
    fill = jnp.zeros((1, BAND - total), jnp.int32)
    own_ref[...] = jnp.concatenate([partner[:, 0:1], fill[:, : total - 1], kept, fill[:, : BAND - 2 * total]], axis=1)
    row = lax.broadcasted_iota(jnp.int32, (rows, BAND), 0)
    notes = jnp.zeros((rows, BAND), jnp.int32)
    for place, values in ((0, kept >> 3), (1, kept & BINS_DEV - 1)):
        notes = jnp.where(row == place, jnp.concatenate([values, fill], axis=1), notes)
    for at in range(windows):
        c, w = at // nwin, at % nwin
        notes = jnp.where(row == rows - windows + at, valid[c, w], notes)
    for h in range(2):
        raw_ref[h, windows] = notes.astype(jnp.float32).astype(jnp.bfloat16)
    for copy in copies[4:]:
        copy.wait()


def bins_of(notes, count):
    digits = notes.astype(jnp.float32).astype(jnp.int32)
    return digits[0:1, 0:count] * BINS_DEV + digits[1:2, 0:count]


def valid_of(notes, windows, at):
    row = notes.shape[0] - windows + at
    return notes[row : row + 1, :]


def whiten(raw, valid, split):
    split[...] = raw.astype(jnp.float32)
    bands = split.shape[0] // 2
    real = split[pl.ds(0, bands, stride=2), :]
    imag = split[pl.ds(1, bands, stride=2), :]
    mean = jnp.sum(real * real + imag * imag, axis=-1, keepdims=True) * (1.0 / BAND)
    gain = lax.rsqrt(mean + 1e-06) * valid
    return [(part * gain).astype(jnp.bfloat16) for part in (real, imag)]


def cross_spectrum(left, right):
    real = imag = 0.0
    for (left_real, left_imag), (right_real, right_imag) in zip(left, right):
        real += left_real * right_real + left_imag * right_imag
        imag += left_imag * right_real - left_real * right_imag
    return [(part * (1.0 / len(left))).astype(jnp.bfloat16) for part in (real, imag)]


def lag_lines(table, spec, twiddle_ref, final, turned, numbers, lines, stride):
    nm = twiddle_ref.shape[1]
    cos, sin = twiddle_ref[0], twiddle_ref[1]
    out = jnp.dot(table, spec, preferred_element_type=jnp.float32)
    for at in range(len(numbers)):
        real = out[:nm, at * BAND : (at + 1) * BAND]
        imag = out[nm:, at * BAND : (at + 1) * BAND]
        turned[at * nm : (at + 1) * nm, 0:BAND] = (real * cos - imag * sin).astype(jnp.bfloat16)
        turned[at * nm : (at + 1) * nm, BAND : 2 * BAND] = (real * sin + imag * cos).astype(jnp.bfloat16)
    corr = lax.dot_general(final, turned[...], (((1,), (1,)), ((), ())), preferred_element_type=jnp.float32)
    nq = corr.shape[0] // 3
    low = lax.broadcasted_iota(jnp.int32, (nq, BAND), 1) < nm
    for at in range(0, len(numbers), 2):
        even, odd, beyond = (corr[k * nq : (k + 1) * nq, at * nm : (at + 2) * nm] for k in range(3))
        lines[pl.ds(numbers[at], nq, stride=stride), :] = jnp.where(low, even, pltpu.roll(odd, nm, 1))
        lines[pl.ds(numbers[at + 1], nq, stride=stride), :] = jnp.where(low, pltpu.roll(even, nm, 1), odd)
        for k in range(2):
            row = nq * stride + numbers[at + k]
            lines[row : row + 1, :] = (pltpu.roll(beyond, nm, 1) if k else beyond)[0:1, :]


def self_kernel(raw_ref, basis_ref, twiddle_ref, white_ref, lines_ref, split, spec, turned, *, nchan, nwin):
    half = white_ref.shape[2]
    lines_ref[...] = jnp.zeros(lines_ref.shape, jnp.float32)
    notes = raw_ref[0, nchan * nwin].astype(jnp.float32)
    for h in range(2):
        for at in range(nchan * nwin):
            valid = valid_of(notes, nchan * nwin, at)
            white = whiten(raw_ref[h, at], valid, split.at[h * nchan * nwin + at])
            for i in range(2):
                white_ref[h, 2 * at + i] = white[i]
        channels = [
            [[white_ref[h, 2 * (c * nwin + w) + i].astype(jnp.float32) for i in range(2)] for w in range(nwin)]
            for c in range(nchan)
        ]
        for at, (a, b) in enumerate(self_pairs(nchan)):
            real, imag = cross_spectrum(channels[a], channels[b])
            spec[2 * h * half : (2 * h + 1) * half, at * BAND : (at + 1) * BAND] = real
            spec[(2 * h + 1) * half : (2 * h + 2) * half, at * BAND : (at + 1) * BAND] = imag
    numbers = range(len(self_pairs(nchan)))
    nm = twiddle_ref.shape[1]
    lag_lines(
        basis_ref[0 : 2 * nm, 0:nm], spec[...], twiddle_ref, basis_ref[2 * nm :, :], turned, numbers, lines_ref, nchan * nchan
    )


def reversed_bits(value, bits):
    return sum((value >> k & 1) << bits - 1 - k for k in range(bits))


def stack_kernel(
    part_ref,
    white_ref,
    self_ref,
    own_ref,
    table_ref,
    basis_ref,
    twiddle_ref,
    keep_ref,
    send_ref,
    split,
    spec,
    turned,
    lines,
    *,
    nblocks,
    nchan,
    nwin,
):
    me = lax.axis_index("chan")
    half = white_ref.shape[1]
    square = nchan * nchan
    nq = lines.shape[0] // (2 * square) - 1
    nm = twiddle_ref.shape[1]
    for q in range(nq + 1):
        lines[q * 2 * square : q * 2 * square + square, :] = self_ref[q * square : (q + 1) * square, :]
        if q == nq:
            start = q * 2 * square + square
            lines[start : start + square, :] = jnp.zeros((square, BAND), jnp.float32)
    others = []
    notes = part_ref[nchan * nwin].astype(jnp.float32)
    for b in range(nchan):
        windows = [
            whiten(part_ref[at], valid_of(notes, nchan * nwin, at), split.at[at])
            for at in range(b * nwin, (b + 1) * nwin)
        ]
        others.append([[part.astype(jnp.float32) for part in parts] for parts in windows])
    for a in range(nchan):
        own = [[white_ref[2 * (a * nwin + w) + i].astype(jnp.float32) for i in range(2)] for w in range(nwin)]
        for b in range(nchan):
            real, imag = cross_spectrum(own, others[b])
            spec[a, 0:half, b * BAND : (b + 1) * BAND] = real
            spec[a, half : 2 * half, b * BAND : (b + 1) * BAND] = imag
    for a in range(nchan):
        numbers = [square + a * nchan + b for b in range(nchan)]
        lag_lines(
            table_ref[...], spec[a], twiddle_ref, basis_ref[2 * nm :, :], turned.at[a], numbers, lines, 2 * square
        )
    exact = [lines[q * 2 * square : (q + 1) * 2 * square, :] for q in range(nq + 1)]
    forward = [block.astype(jnp.bfloat16) for block in exact]
    negated = jnp.dot(
        jnp.concatenate([forward[nq - 1 - q] for q in range(nq)], axis=0),
        basis_ref[0:BAND, BAND : 2 * BAND],
        preferred_element_type=jnp.float32,
    )
    lane = lax.broadcasted_iota(jnp.int32, exact[0].shape, 1)
    backward = [
        jnp.where(lane == 0, exact[nq - q], negated[q * 2 * square : (q + 1) * 2 * square, :]).astype(jnp.bfloat16)
        for q in range(nq)
    ]
    both = jnp.concatenate([jnp.concatenate(parts, axis=1) for parts in (forward[:nq], backward)], axis=0)

    bits = nblocks.bit_length() - 1
    chunk = min(nblocks // 2, 8)
    total = 2 * square
    bins = jnp.concatenate([own_ref[0:1, total : 2 * total], bins_of(part_ref[nchan * nwin], total)], axis=1)
    target = jnp.where(bins >= 0, bins ^ (me * BINS_DEV), -1)
    for out_ref, base in ((keep_ref, 0), (send_ref, nblocks // 2)):

        def add(index, _, out_ref=out_ref, base=base):
            place = lax.broadcasted_iota(jnp.int32, (chunk * BINS_DEV, 4 * square), 0) + (
                (base + index * chunk) * BINS_DEV
            )
            owned = (reversed_bits(place >> 3, bits) << 3) + (place & BINS_DEV - 1)
            chosen = (owned == target).astype(jnp.float32).astype(jnp.bfloat16)
            chosen = jnp.dot(chosen, basis_ref[0 : 4 * square, nm : 2 * nm], preferred_element_type=jnp.float32).astype(jnp.bfloat16)
            sums = jnp.dot(chosen, both, preferred_element_type=jnp.float32)
            for block in range(chunk):
                for q in range(0, nq, 2):
                    tile = jnp.concatenate(
                        [
                            sums[block * BINS_DEV : (block + 1) * BINS_DEV, k * BAND : (k + 1) * BAND]
                            for k in (q, q + 1)
                        ],
                        axis=0,
                    )
                    start = (index * chunk + block) * nq * BINS_DEV + q * BINS_DEV
                    if not isinstance(start, int):
                        start = pl.multiple_of(start, 2 * BINS_DEV)
                    out_ref[pl.ds(start, 2 * BINS_DEV), :] = tile.astype(out_ref.dtype)

        count = nblocks // 2 // chunk
        if count == 1:
            add(0, None)
        else:
            lax.fori_loop(0, count, add, None)


def swap(values, axis, mask):
    return lax.ppermute(values, axis, [(p, p ^ mask) for p in range(lax.axis_size(axis))])


def on_device(spectra, valid, partner, pair_bin, pair_count):
    nblocks = lax.axis_size("chan")
    nchan, nwin, _, nfreq = spectra.shape
    nbands = nfreq // BAND
    half = nbands // 2
    nm = 2 * nbands
    nq = LAGS // nm // 2
    square = nchan * nchan
    windows = nchan * nwin
    npairs = len(self_pairs(nchan))
    me = lax.axis_index("chan")
    raw = spectra.reshape(windows, 2, nbands, BAND).transpose(0, 2, 1, 3).reshape(windows, 2 * nbands, BAND)
    basis, twiddle = tables(nbands, nchan)
    vmem = pl.BlockSpec(memory_space=pltpu.VMEM)
    hbm = pl.BlockSpec(memory_space=pltpu.HBM)
    params = pltpu.CompilerParams(vmem_limit_bytes=32 * 1024 * 1024)

    raw, own = pl.pallas_call(
        prepare_kernel,
        out_shape=[
            jax.ShapeDtypeStruct((2, windows + 1, nbands, BAND), jnp.bfloat16),
            jax.ShapeDtypeStruct((1, BAND), jnp.int32),
        ],
        in_specs=[hbm] * 5,
        out_specs=[vmem] * 2,
        scratch_shapes=[
            pltpu.SMEM(valid.shape, jnp.int32),
            pltpu.VMEM((1, nblocks), jnp.int32),
            pltpu.VMEM((1, pair_bin.shape[0]), jnp.int32),
            pltpu.SMEM((1,), jnp.int32),
            pltpu.SemaphoreType.DMA((6,)),
        ],
    )(raw, valid, partner.reshape(1, -1), pair_bin.reshape(1, -1), pair_count)

    def own_lines(raw, upper):
        white, lines = pl.pallas_call(
            functools.partial(self_kernel, nchan=nchan, nwin=nwin),
            out_shape=[
                jax.ShapeDtypeStruct((2, 2 * windows, half, BAND), jnp.bfloat16),
                jax.ShapeDtypeStruct(((nq + 1) * square, BAND), jnp.float32),
            ],
            in_specs=[vmem] * 3,
            out_specs=[vmem] * 2,
            scratch_shapes=[
                pltpu.VMEM((2 * windows, nbands, BAND), jnp.float32),
                pltpu.VMEM((nm, npairs * BAND), jnp.bfloat16),
                pltpu.VMEM((npairs * nm, 2 * BAND), jnp.bfloat16),
            ],
            compiler_params=params,
        )(raw, basis, twiddle)
        table = lax.dynamic_slice(basis, (0, upper * nbands), (2 * nm, nbands))
        return lax.dynamic_index_in_dim(white, upper, 0, keepdims=False), lines, table

    def stack(part, white, lines, table, own):
        rows = nblocks // 2 * BINS_DEV * nq
        keep, send = pl.pallas_call(
            functools.partial(stack_kernel, nblocks=nblocks, nchan=nchan, nwin=nwin),
            out_shape=[
                jax.ShapeDtypeStruct((rows, BAND), jnp.float32),
                jax.ShapeDtypeStruct((rows, BAND), jnp.bfloat16),
            ],
            in_specs=[vmem] * 7,
            out_specs=[vmem] * 2,
            scratch_shapes=[
                pltpu.VMEM((windows, nbands, BAND), jnp.float32),
                pltpu.VMEM((nchan, nbands, nchan * BAND), jnp.bfloat16),
                pltpu.VMEM((nchan, nchan * nm, 2 * BAND), jnp.bfloat16),
                pltpu.VMEM(((nq + 1) * 2 * square, BAND), jnp.float32),
            ],
            compiler_params=params,
        )(part, white, lines, own, table, basis, twiddle)

        return keep, send

    def branch(mask, raw, own):
        upper = me >> mask.bit_length() - 1 & 1
        part = swap(lax.dynamic_index_in_dim(raw, 1 - upper, 0, keepdims=False), "chan", mask)
        return stack(part, *own_lines(raw, upper), own)

    round_mask = own[0, 0]
    if nblocks <= 16:
        branches = [functools.partial(branch, mask) for mask in range(1, nblocks)]
        keep, send = lax.switch(round_mask - 1, branches, raw, own)
    else:
        upper = ((me ^ round_mask) < me).astype(jnp.int32)
        part = lax.dynamic_index_in_dim(raw, 1 - upper, 0, keepdims=False)
        for bit in range(nblocks.bit_length() - 1):
            part = jnp.where(round_mask >> bit & 1 == 1, swap(part, "chan", 1 << bit), part)
        keep, send = stack(part, *own_lines(raw, upper), own)

    sums = keep + swap(send, "chan", 1).astype(jnp.float32)
    mask = 2
    while mask < nblocks:
        rows = sums.shape[0] // 2
        received = swap(sums[rows:].astype(jnp.bfloat16), "chan", mask)
        sums = sums[:rows] + received.astype(jnp.float32)
        mask *= 2
    return sums.reshape(nq, BINS_DEV, BAND).transpose(1, 0, 2).reshape(BINS_DEV, LAGS)


def solution(mesh):
    in_specs = (
        P(("grp", "chan"), None, None, None),
        P(("grp", "chan"), None),
        P(),
        P(("grp", "chan")),
        P(("grp", "chan")),
    )
    out_specs = P(("grp", "chan"), None)
    return jax.shard_map(
        on_device, mesh=mesh, in_specs=in_specs, out_specs=out_specs, check_vma=False
    )
```

```python
import functools
import math

import jax
import jax.numpy as jnp
import numpy as np
from jax import lax
from jax.experimental import pallas as pl
from jax.experimental.pallas import tpu as pltpu
from jax.sharding import PartitionSpec as P

BAND = 128
LAGS = 1024
BINS_DEV = 8
PAIRS_DEV = 32


def self_pairs(nchan):
    return [(a, b) for a in range(nchan) for b in range(a + 1, nchan)]


def tables(nbands, nchan):
    nfreq = nbands * BAND
    half = nbands // 2
    nm = 2 * nbands
    nq = LAGS // nm
    square = nchan * nchan
    m = np.arange(nm)
    first = 2.0 * np.pi * ((m[:, None] * np.arange(nbands)[None, :]) % nm) / nm
    cos, sin = np.cos(first), np.sin(first)
    order = np.concatenate([np.arange(0, nq, 2), np.arange(1, nq, 2), np.full(nq // 2, nq)]) - nq // 2
    last = 2.0 * np.pi * ((order[:, None] * np.arange(BAND)[None, :]) % BAND) / BAND
    basis = np.zeros((2 * nm + 3 * nq // 2, 2 * BAND))
    for h in range(2):
        part = slice(h * half, (h + 1) * half)
        at = h * nbands
        basis[:nm, at : at + nbands] = np.concatenate([cos[:, part], -sin[:, part]], axis=1)
        basis[nm : 2 * nm, at : at + nbands] = np.concatenate([sin[:, part], cos[:, part]], axis=1)
    for line, (a, b) in enumerate(self_pairs(nchan)):
        basis[a * nchan + b, nm + line] = 1
        basis[b * nchan + a, nm + 2 * square + line] = 1
    for a in range(nchan):
        for b in range(nchan):
            line = square + a * nchan + b
            basis[line, nm + line] = 1
            basis[3 * square + b * nchan + a, nm + 2 * square + line] = 1
    lane = np.arange(1, BAND)
    basis[BAND - lane, BAND + lane] = 1
    basis[2 * nm :] = np.concatenate([np.cos(last), -np.sin(last)], axis=1)
    scale = 1.0 / math.sqrt(nfreq) / math.sqrt(PAIRS_DEV // BINS_DEV)
    angle = 2.0 * np.pi * (m[:, None] * np.arange(BAND)[None, :]) / (2 * nfreq)
    twiddle = np.stack([np.cos(angle), np.sin(angle)]) * scale
    return jnp.asarray(basis, jnp.bfloat16), jnp.asarray(twiddle, jnp.float32)


def prepare_kernel(
    raw_hbm, valid_hbm, partner_hbm, bins_hbm, count_hbm, raw_ref, own_ref, valid, partner, bins, count, sems
):
    nchan, nwin = valid.shape
    windows, rows = raw_hbm.shape[0], raw_ref.shape[2]
    moves = [(bins_hbm, bins), (count_hbm, count), (valid_hbm, valid), (partner_hbm, partner)]
    moves += [(raw_hbm.at[:, h * rows : (h + 1) * rows, :], raw_ref.at[h, 0:windows]) for h in range(2)]
    copies = [pltpu.make_async_copy(source, target, sems.at[k]) for k, (source, target) in enumerate(moves)]
    for copy in copies:
        copy.start()
    for copy in copies[:4]:
        copy.wait()
    number = lax.broadcasted_iota(jnp.int32, bins.shape, 1)
    kept = jnp.where(number < count[0], bins[...], -1)
    total = kept.shape[1]
    fill = jnp.zeros((1, BAND - total), jnp.int32)
    own_ref[...] = jnp.concatenate([partner[:, 0:1], fill[:, : total - 1], kept, fill[:, : BAND - 2 * total]], axis=1)
    row = lax.broadcasted_iota(jnp.int32, (rows, BAND), 0)
    notes = jnp.zeros((rows, BAND), jnp.int32)
    for place, values in ((0, kept >> 3), (1, kept & BINS_DEV - 1)):
        notes = jnp.where(row == place, jnp.concatenate([values, fill], axis=1), notes)
    for at in range(windows):
        c, w = at // nwin, at % nwin
        notes = jnp.where(row == rows - windows + at, valid[c, w], notes)
    for h in range(2):
        raw_ref[h, windows] = notes.astype(jnp.float32).astype(jnp.bfloat16)
    for copy in copies[4:]:
        copy.wait()


def bins_of(notes, count):
    digits = notes.astype(jnp.float32).astype(jnp.int32)
    return digits[0:1, 0:count] * BINS_DEV + digits[1:2, 0:count]


def valid_of(notes, windows, at):
    row = notes.shape[0] - windows + at
    return notes[row : row + 1, :]


def whiten(raw, valid, split):
    split[...] = raw.astype(jnp.float32)
    bands = split.shape[0] // 2
    real = split[pl.ds(0, bands, stride=2), :]
    imag = split[pl.ds(1, bands, stride=2), :]
    mean = jnp.sum(real * real + imag * imag, axis=-1, keepdims=True) * (1.0 / BAND)
    gain = lax.rsqrt(mean + 1e-06) * valid
    return [(part * gain).astype(jnp.bfloat16) for part in (real, imag)]


def cross_spectrum(left, right):
    real = imag = 0.0
    for (left_real, left_imag), (right_real, right_imag) in zip(left, right):
        real += left_real * right_real + left_imag * right_imag
        imag += left_imag * right_real - left_real * right_imag
    return [(part * (1.0 / len(left))).astype(jnp.bfloat16) for part in (real, imag)]


def lag_lines(table, spec, twiddle_ref, final, turned, numbers, lines, stride):
    nm = twiddle_ref.shape[1]
    cos, sin = twiddle_ref[0], twiddle_ref[1]
    out = jnp.dot(table, spec, preferred_element_type=jnp.float32)
    for at in range(len(numbers)):
        real = out[:nm, at * BAND : (at + 1) * BAND]
        imag = out[nm:, at * BAND : (at + 1) * BAND]
        turned[at * nm : (at + 1) * nm, 0:BAND] = (real * cos - imag * sin).astype(jnp.bfloat16)
        turned[at * nm : (at + 1) * nm, BAND : 2 * BAND] = (real * sin + imag * cos).astype(jnp.bfloat16)
    corr = lax.dot_general(final, turned[...], (((1,), (1,)), ((), ())), preferred_element_type=jnp.float32)
    nq = corr.shape[0] // 3
    low = lax.broadcasted_iota(jnp.int32, (nq, BAND), 1) < nm
    for at in range(0, len(numbers), 2):
        even, odd, beyond = (corr[k * nq : (k + 1) * nq, at * nm : (at + 2) * nm] for k in range(3))
        lines[pl.ds(numbers[at], nq, stride=stride), :] = jnp.where(low, even, pltpu.roll(odd, nm, 1))
        lines[pl.ds(numbers[at + 1], nq, stride=stride), :] = jnp.where(low, pltpu.roll(even, nm, 1), odd)
        for k in range(2):
            row = nq * stride + numbers[at + k]
            lines[row : row + 1, :] = (pltpu.roll(beyond, nm, 1) if k else beyond)[0:1, :]


def self_kernel(raw_ref, basis_ref, twiddle_ref, white_ref, lines_ref, split, spec, turned, *, nchan, nwin):
    half = white_ref.shape[2]
    lines_ref[...] = jnp.zeros(lines_ref.shape, jnp.float32)
    notes = raw_ref[0, nchan * nwin].astype(jnp.float32)
    for h in range(2):
        for at in range(nchan * nwin):
            valid = valid_of(notes, nchan * nwin, at)
            white = whiten(raw_ref[h, at], valid, split.at[h * nchan * nwin + at])
            for i in range(2):
                white_ref[h, 2 * at + i] = white[i]
        channels = [
            [[white_ref[h, 2 * (c * nwin + w) + i].astype(jnp.float32) for i in range(2)] for w in range(nwin)]
            for c in range(nchan)
        ]
        for at, (a, b) in enumerate(self_pairs(nchan)):
            real, imag = cross_spectrum(channels[a], channels[b])
            spec[2 * h * half : (2 * h + 1) * half, at * BAND : (at + 1) * BAND] = real
            spec[(2 * h + 1) * half : (2 * h + 2) * half, at * BAND : (at + 1) * BAND] = imag
    numbers = range(len(self_pairs(nchan)))
    nm = twiddle_ref.shape[1]
    lag_lines(
        basis_ref[0 : 2 * nm, 0:nm], spec[...], twiddle_ref, basis_ref[2 * nm :, :], turned, numbers, lines_ref, nchan * nchan
    )


def reversed_bits(value, bits):
    return sum((value >> k & 1) << bits - 1 - k for k in range(bits))


def stack_kernel(
    part_ref,
    white_ref,
    self_ref,
    own_ref,
    table_ref,
    basis_ref,
    twiddle_ref,
    keep_ref,
    send_ref,
    split,
    spec,
    turned,
    lines,
    *,
    nblocks,
    nchan,
    nwin,
):
    me = lax.axis_index("chan")
    half = white_ref.shape[1]
    square = nchan * nchan
    nq = lines.shape[0] // (2 * square) - 1
    nm = twiddle_ref.shape[1]
    for q in range(nq + 1):
        lines[q * 2 * square : q * 2 * square + square, :] = self_ref[q * square : (q + 1) * square, :]
        if q == nq:
            start = q * 2 * square + square
            lines[start : start + square, :] = jnp.zeros((square, BAND), jnp.float32)
    others = []
    notes = part_ref[nchan * nwin].astype(jnp.float32)
    for b in range(nchan):
        windows = [
            whiten(part_ref[at], valid_of(notes, nchan * nwin, at), split.at[at])
            for at in range(b * nwin, (b + 1) * nwin)
        ]
        others.append([[part.astype(jnp.float32) for part in parts] for parts in windows])
    for a in range(nchan):
        own = [[white_ref[2 * (a * nwin + w) + i].astype(jnp.float32) for i in range(2)] for w in range(nwin)]
        for b in range(nchan):
            real, imag = cross_spectrum(own, others[b])
            spec[a, 0:half, b * BAND : (b + 1) * BAND] = real
            spec[a, half : 2 * half, b * BAND : (b + 1) * BAND] = imag
    for a in range(nchan):
        numbers = [square + a * nchan + b for b in range(nchan)]
        lag_lines(
            table_ref[...], spec[a], twiddle_ref, basis_ref[2 * nm :, :], turned.at[a], numbers, lines, 2 * square
        )
    exact = [lines[q * 2 * square : (q + 1) * 2 * square, :] for q in range(nq + 1)]
    forward = [block.astype(jnp.bfloat16) for block in exact]
    negated = jnp.dot(
        jnp.concatenate([forward[nq - 1 - q] for q in range(nq)], axis=0),
        basis_ref[0:BAND, BAND : 2 * BAND],
        preferred_element_type=jnp.float32,
    )
    lane = lax.broadcasted_iota(jnp.int32, exact[0].shape, 1)
    backward = [
        jnp.where(lane == 0, exact[nq - q], negated[q * 2 * square : (q + 1) * 2 * square, :]).astype(jnp.bfloat16)
        for q in range(nq)
    ]
    both = jnp.concatenate([jnp.concatenate(parts, axis=1) for parts in (forward[:nq], backward)], axis=0)

    bits = nblocks.bit_length() - 1
    chunk = min(nblocks // 2, 8)
    total = 2 * square
    bins = jnp.concatenate([own_ref[0:1, total : 2 * total], bins_of(part_ref[nchan * nwin], total)], axis=1)
    target = jnp.where(bins >= 0, bins ^ (me * BINS_DEV), -1)
    for out_ref, base in ((keep_ref, 0), (send_ref, nblocks // 2)):

        def add(index, _, out_ref=out_ref, base=base):
            place = lax.broadcasted_iota(jnp.int32, (chunk * BINS_DEV, 4 * square), 0) + (
                (base + index * chunk) * BINS_DEV
            )
            owned = (reversed_bits(place >> 3, bits) << 3) + (place & BINS_DEV - 1)
            chosen = (owned == target).astype(jnp.float32).astype(jnp.bfloat16)
            chosen = jnp.dot(chosen, basis_ref[0 : 4 * square, nm : 2 * nm], preferred_element_type=jnp.float32).astype(jnp.bfloat16)
            sums = jnp.dot(chosen, both, preferred_element_type=jnp.float32)
            for block in range(chunk):
                for q in range(0, nq, 2):
                    tile = jnp.concatenate(
                        [
                            sums[block * BINS_DEV : (block + 1) * BINS_DEV, k * BAND : (k + 1) * BAND]
                            for k in (q, q + 1)
                        ],
                        axis=0,
                    )
                    start = (index * chunk + block) * nq * BINS_DEV + q * BINS_DEV
                    if not isinstance(start, int):
                        start = pl.multiple_of(start, 2 * BINS_DEV)
                    out_ref[pl.ds(start, 2 * BINS_DEV), :] = tile.astype(out_ref.dtype)

        count = nblocks // 2 // chunk
        if count == 1:
            add(0, None)
        else:
            lax.fori_loop(0, count, add, None)


def swap(values, axis, mask):
    return lax.ppermute(values, axis, [(p, p ^ mask) for p in range(lax.axis_size(axis))])


def on_device(spectra, valid, partner, pair_bin, pair_count):
    nblocks = lax.axis_size("chan")
    nchan, nwin, _, nfreq = spectra.shape
    nbands = nfreq // BAND
    half = nbands // 2
    nm = 2 * nbands
    nq = LAGS // nm // 2
    square = nchan * nchan
    windows = nchan * nwin
    npairs = len(self_pairs(nchan))
    me = lax.axis_index("chan")
    raw = spectra.reshape(windows, 2, nbands, BAND).transpose(0, 2, 1, 3).reshape(windows, 2 * nbands, BAND)
    basis, twiddle = tables(nbands, nchan)
    vmem = pl.BlockSpec(memory_space=pltpu.VMEM)
    hbm = pl.BlockSpec(memory_space=pltpu.HBM)
    params = pltpu.CompilerParams(vmem_limit_bytes=32 * 1024 * 1024)

    raw, own = pl.pallas_call(
        prepare_kernel,
        out_shape=[
            jax.ShapeDtypeStruct((2, windows + 1, nbands, BAND), jnp.bfloat16),
            jax.ShapeDtypeStruct((1, BAND), jnp.int32),
        ],
        in_specs=[hbm] * 5,
        out_specs=[vmem] * 2,
        scratch_shapes=[
            pltpu.SMEM(valid.shape, jnp.int32),
            pltpu.VMEM((1, nblocks), jnp.int32),
            pltpu.VMEM((1, pair_bin.shape[0]), jnp.int32),
            pltpu.SMEM((1,), jnp.int32),
            pltpu.SemaphoreType.DMA((6,)),
        ],
    )(raw, valid, partner.reshape(1, -1), pair_bin.reshape(1, -1), pair_count)

    def own_lines(raw, upper):
        white, lines = pl.pallas_call(
            functools.partial(self_kernel, nchan=nchan, nwin=nwin),
            out_shape=[
                jax.ShapeDtypeStruct((2, 2 * windows, half, BAND), jnp.bfloat16),
                jax.ShapeDtypeStruct(((nq + 1) * square, BAND), jnp.float32),
            ],
            in_specs=[vmem] * 3,
            out_specs=[vmem] * 2,
            scratch_shapes=[
                pltpu.VMEM((2 * windows, nbands, BAND), jnp.float32),
                pltpu.VMEM((nm, npairs * BAND), jnp.bfloat16),
                pltpu.VMEM((npairs * nm, 2 * BAND), jnp.bfloat16),
            ],
            compiler_params=params,
        )(raw, basis, twiddle)
        table = lax.dynamic_slice(basis, (0, upper * nbands), (2 * nm, nbands))
        return lax.dynamic_index_in_dim(white, upper, 0, keepdims=False), lines, table

    def stacked(part, white, lines, table, own):
        rows = nblocks // 2 * BINS_DEV * nq
        keep, send = pl.pallas_call(
            functools.partial(stack_kernel, nblocks=nblocks, nchan=nchan, nwin=nwin),
            out_shape=[
                jax.ShapeDtypeStruct((rows, BAND), jnp.float32),
                jax.ShapeDtypeStruct((rows, BAND), jnp.bfloat16),
            ],
            in_specs=[vmem] * 7,
            out_specs=[vmem] * 2,
            scratch_shapes=[
                pltpu.VMEM((windows, nbands, BAND), jnp.float32),
                pltpu.VMEM((nchan, nbands, nchan * BAND), jnp.bfloat16),
                pltpu.VMEM((nchan, nchan * nm, 2 * BAND), jnp.bfloat16),
                pltpu.VMEM(((nq + 1) * 2 * square, BAND), jnp.float32),
            ],
            compiler_params=params,
        )(part, white, lines, own, table, basis, twiddle)

        sums = keep + swap(send, "chan", 1).astype(jnp.float32)
        mask = 2
        while mask < nblocks:
            rows = sums.shape[0] // 2
            received = swap(sums[rows:].astype(jnp.bfloat16), "chan", mask)
            sums = sums[:rows] + received.astype(jnp.float32)
            mask *= 2
        return sums.reshape(nq, BINS_DEV, BAND).transpose(1, 0, 2).reshape(BINS_DEV, LAGS)

    def branch(mask, raw, own):
        upper = me >> mask.bit_length() - 1 & 1
        part = swap(lax.dynamic_index_in_dim(raw, 1 - upper, 0, keepdims=False), "chan", mask)
        return stacked(part, *own_lines(raw, upper), own)

    round_mask = own[0, 0]
    if nblocks <= 16:
        branches = [functools.partial(branch, mask) for mask in range(1, nblocks)]
        result = lax.switch(round_mask - 1, branches, raw, own)
    else:
        upper = ((me ^ round_mask) < me).astype(jnp.int32)
        part = lax.dynamic_index_in_dim(raw, 1 - upper, 0, keepdims=False)
        for bit in range(nblocks.bit_length() - 1):
            part = jnp.where(round_mask >> bit & 1 == 1, swap(part, "chan", 1 << bit), part)
        result = stacked(part, *own_lines(raw, upper), own)

    return result


def solution(mesh):
    in_specs = (
        P(("grp", "chan"), None, None, None),
        P(("grp", "chan"), None),
        P(),
        P(("grp", "chan")),
        P(("grp", "chan")),
    )
    out_specs = P(("grp", "chan"), None)
    return jax.shard_map(
        on_device, mesh=mesh, in_specs=in_specs, out_specs=out_specs, check_vma=False
    )
```

```python
import functools
import math

import jax
import jax.numpy as jnp
import numpy as np
from jax import lax
from jax.experimental import pallas as pl
from jax.experimental.pallas import tpu as pltpu
from jax.sharding import PartitionSpec as P

BAND = 128
LAGS = 1024
BINS_DEV = 8
PAIRS_DEV = 32


def self_pairs(nchan):
    return [(a, b) for a in range(nchan) for b in range(a + 1, nchan)]


def tables(nbands, nchan):
    nfreq = nbands * BAND
    half = nbands // 2
    nm = 2 * nbands
    nq = LAGS // nm
    square = nchan * nchan
    m = np.arange(nm)
    first = 2.0 * np.pi * ((m[:, None] * np.arange(nbands)[None, :]) % nm) / nm
    cos, sin = np.cos(first), np.sin(first)
    order = np.concatenate([np.arange(0, nq, 2), np.arange(1, nq, 2), np.full(nq // 2, nq)]) - nq // 2
    last = 2.0 * np.pi * ((order[:, None] * np.arange(BAND)[None, :]) % BAND) / BAND
    basis = np.zeros((2 * nm + 3 * nq // 2, 2 * BAND))
    for h in range(2):
        part = slice(h * half, (h + 1) * half)
        at = h * nbands
        basis[:nm, at : at + nbands] = np.concatenate([cos[:, part], -sin[:, part]], axis=1)
        basis[nm : 2 * nm, at : at + nbands] = np.concatenate([sin[:, part], cos[:, part]], axis=1)
    for line, (a, b) in enumerate(self_pairs(nchan)):
        basis[a * nchan + b, nm + line] = 1
        basis[b * nchan + a, nm + 2 * square + line] = 1
    for a in range(nchan):
        for b in range(nchan):
            line = square + a * nchan + b
            basis[line, nm + line] = 1
            basis[3 * square + b * nchan + a, nm + 2 * square + line] = 1
    lane = np.arange(1, BAND)
    basis[BAND - lane, BAND + lane] = 1
    basis[2 * nm :] = np.concatenate([np.cos(last), -np.sin(last)], axis=1)
    scale = 1.0 / math.sqrt(nfreq) / math.sqrt(PAIRS_DEV // BINS_DEV)
    angle = 2.0 * np.pi * (m[:, None] * np.arange(BAND)[None, :]) / (2 * nfreq)
    twiddle = np.stack([np.cos(angle), np.sin(angle)]) * scale
    return jnp.asarray(basis, jnp.bfloat16), jnp.asarray(twiddle, jnp.float32)


def prepare_kernel(
    raw_hbm, valid_hbm, partner_hbm, bins_hbm, count_hbm, raw_ref, own_ref, valid, partner, bins, count, sems
):
    nchan, nwin = valid.shape
    windows, rows = raw_hbm.shape[0], raw_ref.shape[2]
    moves = [(bins_hbm, bins), (count_hbm, count), (valid_hbm, valid), (partner_hbm, partner)]
    moves += [(raw_hbm.at[:, h * rows : (h + 1) * rows, :], raw_ref.at[h, 0:windows]) for h in range(2)]
    copies = [pltpu.make_async_copy(source, target, sems.at[k]) for k, (source, target) in enumerate(moves)]
    for copy in copies:
        copy.start()
    for copy in copies[:4]:
        copy.wait()
    number = lax.broadcasted_iota(jnp.int32, bins.shape, 1)
    kept = jnp.where(number < count[0], bins[...], -1)
    total = kept.shape[1]
    fill = jnp.zeros((1, BAND - total), jnp.int32)
    own_ref[...] = jnp.concatenate([partner[:, 0:1], fill[:, : total - 1], kept, fill[:, : BAND - 2 * total]], axis=1)
    row = lax.broadcasted_iota(jnp.int32, (rows, BAND), 0)
    notes = jnp.zeros((rows, BAND), jnp.int32)
    for place, values in ((0, kept >> 3), (1, kept & BINS_DEV - 1)):
        notes = jnp.where(row == place, jnp.concatenate([values, fill], axis=1), notes)
    for at in range(windows):
        c, w = at // nwin, at % nwin
        notes = jnp.where(row == rows - windows + at, valid[c, w], notes)
    for h in range(2):
        raw_ref[h, windows] = notes.astype(jnp.float32).astype(jnp.bfloat16)
    for copy in copies[4:]:
        copy.wait()


def bins_of(notes, count):
    digits = notes.astype(jnp.float32).astype(jnp.int32)
    return digits[0:1, 0:count] * BINS_DEV + digits[1:2, 0:count]


def valid_of(notes, windows, at):
    row = notes.shape[0] - windows + at
    return notes[row : row + 1, :]


def whiten(raw, valid, split):
    split[...] = raw.astype(jnp.float32)
    bands = split.shape[0] // 2
    real = split[pl.ds(0, bands, stride=2), :]
    imag = split[pl.ds(1, bands, stride=2), :]
    mean = jnp.sum(real * real + imag * imag, axis=-1, keepdims=True) * (1.0 / BAND)
    gain = lax.rsqrt(mean + 1e-06) * valid
    return [(part * gain).astype(jnp.bfloat16) for part in (real, imag)]


def cross_spectrum(left, right):
    real = imag = 0.0
    for (left_real, left_imag), (right_real, right_imag) in zip(left, right):
        real += left_real * right_real + left_imag * right_imag
        imag += left_imag * right_real - left_real * right_imag
    return [(part * (1.0 / len(left))).astype(jnp.bfloat16) for part in (real, imag)]


def lag_lines(table, spec, twiddle_ref, final, turned, numbers, lines, stride):
    nm = twiddle_ref.shape[1]
    cos, sin = twiddle_ref[0], twiddle_ref[1]
    out = jnp.dot(table, spec, preferred_element_type=jnp.float32)
    for at in range(len(numbers)):
        real = out[:nm, at * BAND : (at + 1) * BAND]
        imag = out[nm:, at * BAND : (at + 1) * BAND]
        turned[at * nm : (at + 1) * nm, 0:BAND] = (real * cos - imag * sin).astype(jnp.bfloat16)
        turned[at * nm : (at + 1) * nm, BAND : 2 * BAND] = (real * sin + imag * cos).astype(jnp.bfloat16)
    corr = lax.dot_general(final, turned[...], (((1,), (1,)), ((), ())), preferred_element_type=jnp.float32)
    nq = corr.shape[0] // 3
    low = lax.broadcasted_iota(jnp.int32, (nq, BAND), 1) < nm
    for at in range(0, len(numbers), 2):
        even, odd, beyond = (corr[k * nq : (k + 1) * nq, at * nm : (at + 2) * nm] for k in range(3))
        lines[pl.ds(numbers[at], nq, stride=stride), :] = jnp.where(low, even, pltpu.roll(odd, nm, 1))
        lines[pl.ds(numbers[at + 1], nq, stride=stride), :] = jnp.where(low, pltpu.roll(even, nm, 1), odd)
        for k in range(2):
            row = nq * stride + numbers[at + k]
            lines[row : row + 1, :] = (pltpu.roll(beyond, nm, 1) if k else beyond)[0:1, :]


def self_kernel(raw_ref, basis_ref, twiddle_ref, white_ref, lines_ref, split, spec, turned, *, nchan, nwin):
    half = white_ref.shape[2]
    lines_ref[...] = jnp.zeros(lines_ref.shape, jnp.float32)
    notes = raw_ref[0, nchan * nwin].astype(jnp.float32)
    for h in range(2):
        for at in range(nchan * nwin):
            valid = valid_of(notes, nchan * nwin, at)
            white = whiten(raw_ref[h, at], valid, split.at[h * nchan * nwin + at])
            for i in range(2):
                white_ref[h, 2 * at + i] = white[i]
        channels = [
            [[white_ref[h, 2 * (c * nwin + w) + i].astype(jnp.float32) for i in range(2)] for w in range(nwin)]
            for c in range(nchan)
        ]
        for at, (a, b) in enumerate(self_pairs(nchan)):
            real, imag = cross_spectrum(channels[a], channels[b])
            spec[2 * h * half : (2 * h + 1) * half, at * BAND : (at + 1) * BAND] = real
            spec[(2 * h + 1) * half : (2 * h + 2) * half, at * BAND : (at + 1) * BAND] = imag
    numbers = range(len(self_pairs(nchan)))
    nm = twiddle_ref.shape[1]
    lag_lines(
        basis_ref[0 : 2 * nm, 0:nm], spec[...], twiddle_ref, basis_ref[2 * nm :, :], turned, numbers, lines_ref, nchan * nchan
    )


def reversed_bits(value, bits):
    return sum((value >> k & 1) << bits - 1 - k for k in range(bits))


def stack_kernel(
    part_ref,
    white_ref,
    self_ref,
    own_ref,
    table_ref,
    basis_ref,
    twiddle_ref,
    keep_ref,
    send_ref,
    split,
    spec,
    turned,
    lines,
    *,
    nblocks,
    nchan,
    nwin,
):
    me = lax.axis_index("chan")
    half = white_ref.shape[1]
    square = nchan * nchan
    nq = lines.shape[0] // (2 * square) - 1
    nm = twiddle_ref.shape[1]
    for q in range(nq + 1):
        lines[q * 2 * square : q * 2 * square + square, :] = self_ref[q * square : (q + 1) * square, :]
        if q == nq:
            start = q * 2 * square + square
            lines[start : start + square, :] = jnp.zeros((square, BAND), jnp.float32)
    others = []
    notes = part_ref[nchan * nwin].astype(jnp.float32)
    for b in range(nchan):
        windows = [
            whiten(part_ref[at], valid_of(notes, nchan * nwin, at), split.at[at])
            for at in range(b * nwin, (b + 1) * nwin)
        ]
        others.append([[part.astype(jnp.float32) for part in parts] for parts in windows])
    for a in range(nchan):
        own = [[white_ref[2 * (a * nwin + w) + i].astype(jnp.float32) for i in range(2)] for w in range(nwin)]
        for b in range(nchan):
            real, imag = cross_spectrum(own, others[b])
            spec[a, 0:half, b * BAND : (b + 1) * BAND] = real
            spec[a, half : 2 * half, b * BAND : (b + 1) * BAND] = imag
    for a in range(nchan):
        numbers = [square + a * nchan + b for b in range(nchan)]
        lag_lines(
            table_ref[...], spec[a], twiddle_ref, basis_ref[2 * nm :, :], turned.at[a], numbers, lines, 2 * square
        )
    exact = [lines[q * 2 * square : (q + 1) * 2 * square, :] for q in range(nq + 1)]
    forward = [block.astype(jnp.bfloat16) for block in exact]
    negated = jnp.dot(
        jnp.concatenate([forward[nq - 1 - q] for q in range(nq)], axis=0),
        basis_ref[0:BAND, BAND : 2 * BAND],
        preferred_element_type=jnp.float32,
    )
    lane = lax.broadcasted_iota(jnp.int32, exact[0].shape, 1)
    backward = [
        jnp.where(lane == 0, exact[nq - q], negated[q * 2 * square : (q + 1) * 2 * square, :]).astype(jnp.bfloat16)
        for q in range(nq)
    ]
    both = jnp.concatenate([jnp.concatenate(parts, axis=1) for parts in (forward[:nq], backward)], axis=0)

    bits = nblocks.bit_length() - 1
    total = 2 * square
    bins = jnp.concatenate([own_ref[0:1, total : 2 * total], bins_of(part_ref[nchan * nwin], total)], axis=1)
    target = jnp.where(bins >= 0, bins ^ (me * BINS_DEV), -1)
    chunk = min(nblocks, 16)

    def add(index, _):
        place = lax.broadcasted_iota(jnp.int32, (chunk * BINS_DEV, 2 * total), 0) + index * chunk * BINS_DEV
        owned = (reversed_bits(place >> 3, bits) << 3) + (place & BINS_DEV - 1)
        chosen = (owned == target).astype(jnp.float32).astype(jnp.bfloat16)
        chosen = jnp.dot(chosen, basis_ref[0 : 2 * total, nm : 2 * nm], preferred_element_type=jnp.float32)
        sums = jnp.dot(chosen.astype(jnp.bfloat16), both, preferred_element_type=jnp.float32)

        def store(out_ref, blocks, first):
            for block in blocks:
                for q in range(0, nq, 2):
                    rows = slice(block * BINS_DEV, (block + 1) * BINS_DEV)
                    tile = jnp.concatenate([sums[rows, k * BAND : (k + 1) * BAND] for k in (q, q + 1)], axis=0)
                    start = ((first + block) * nq + q) * BINS_DEV
                    if not isinstance(start, int):
                        start = pl.multiple_of(start, 2 * BINS_DEV)
                    out_ref[pl.ds(start, 2 * BINS_DEV), :] = tile.astype(out_ref.dtype)

        if nblocks == chunk:
            store(send_ref, range(chunk // 2, chunk), -(chunk // 2))
            store(keep_ref, range(chunk // 2), 0)
        else:
            count = nblocks // 2 // chunk
            pl.when(index < count)(lambda: store(keep_ref, range(chunk), index * chunk))
            pl.when(index >= count)(lambda: store(send_ref, range(chunk), (index - count) * chunk))

    if nblocks == chunk:
        add(0, None)
    else:
        lax.fori_loop(0, nblocks // chunk, add, None)


def swap(values, axis, mask):
    return lax.ppermute(values, axis, [(p, p ^ mask) for p in range(lax.axis_size(axis))])


def on_device(spectra, valid, partner, pair_bin, pair_count):
    nblocks = lax.axis_size("chan")
    nchan, nwin, _, nfreq = spectra.shape
    nbands = nfreq // BAND
    half = nbands // 2
    nm = 2 * nbands
    nq = LAGS // nm // 2
    square = nchan * nchan
    windows = nchan * nwin
    npairs = len(self_pairs(nchan))
    me = lax.axis_index("chan")
    raw = spectra.reshape(windows, 2, nbands, BAND).transpose(0, 2, 1, 3).reshape(windows, 2 * nbands, BAND)
    basis, twiddle = tables(nbands, nchan)
    vmem = pl.BlockSpec(memory_space=pltpu.VMEM)
    hbm = pl.BlockSpec(memory_space=pltpu.HBM)
    params = pltpu.CompilerParams(vmem_limit_bytes=32 * 1024 * 1024)

    raw, own = pl.pallas_call(
        prepare_kernel,
        out_shape=[
            jax.ShapeDtypeStruct((2, windows + 1, nbands, BAND), jnp.bfloat16),
            jax.ShapeDtypeStruct((1, BAND), jnp.int32),
        ],
        in_specs=[hbm] * 5,
        out_specs=[vmem] * 2,
        scratch_shapes=[
            pltpu.SMEM(valid.shape, jnp.int32),
            pltpu.VMEM((1, nblocks), jnp.int32),
            pltpu.VMEM((1, pair_bin.shape[0]), jnp.int32),
            pltpu.SMEM((1,), jnp.int32),
            pltpu.SemaphoreType.DMA((6,)),
        ],
    )(raw, valid, partner.reshape(1, -1), pair_bin.reshape(1, -1), pair_count)

    def own_lines(raw, upper):
        white, lines = pl.pallas_call(
            functools.partial(self_kernel, nchan=nchan, nwin=nwin),
            out_shape=[
                jax.ShapeDtypeStruct((2, 2 * windows, half, BAND), jnp.bfloat16),
                jax.ShapeDtypeStruct(((nq + 1) * square, BAND), jnp.float32),
            ],
            in_specs=[vmem] * 3,
            out_specs=[vmem] * 2,
            scratch_shapes=[
                pltpu.VMEM((2 * windows, nbands, BAND), jnp.float32),
                pltpu.VMEM((nm, npairs * BAND), jnp.bfloat16),
                pltpu.VMEM((npairs * nm, 2 * BAND), jnp.bfloat16),
            ],
            compiler_params=params,
        )(raw, basis, twiddle)
        table = lax.dynamic_slice(basis, (0, upper * nbands), (2 * nm, nbands))
        return lax.dynamic_index_in_dim(white, upper, 0, keepdims=False), lines, table

    def stacked(part, white, lines, table, own):
        rows = nblocks // 2 * BINS_DEV * nq
        keep, send = pl.pallas_call(
            functools.partial(stack_kernel, nblocks=nblocks, nchan=nchan, nwin=nwin),
            out_shape=[
                jax.ShapeDtypeStruct((rows, BAND), jnp.float32),
                jax.ShapeDtypeStruct((rows, BAND), jnp.bfloat16),
            ],
            in_specs=[vmem] * 7,
            out_specs=[vmem] * 2,
            scratch_shapes=[
                pltpu.VMEM((windows, nbands, BAND), jnp.float32),
                pltpu.VMEM((nchan, nbands, nchan * BAND), jnp.bfloat16),
                pltpu.VMEM((nchan, nchan * nm, 2 * BAND), jnp.bfloat16),
                pltpu.VMEM(((nq + 1) * 2 * square, BAND), jnp.float32),
            ],
            compiler_params=params,
        )(part, white, lines, own, table, basis, twiddle)

        sums = keep + swap(send, "chan", 1).astype(jnp.float32)
        mask = 2
        while mask < nblocks:
            rows = sums.shape[0] // 2
            received = swap(sums[rows:].astype(jnp.bfloat16), "chan", mask)
            sums = sums[:rows] + received.astype(jnp.float32)
            mask *= 2
        return sums.reshape(nq, BINS_DEV, BAND).transpose(1, 0, 2).reshape(BINS_DEV, LAGS)

    def branch(mask, raw, own):
        upper = me >> mask.bit_length() - 1 & 1
        part = swap(lax.dynamic_index_in_dim(raw, 1 - upper, 0, keepdims=False), "chan", mask)
        return stacked(part, *own_lines(raw, upper), own)

    round_mask = own[0, 0]
    if nblocks <= 16:
        branches = [functools.partial(branch, mask) for mask in range(1, nblocks)]
        result = lax.switch(round_mask - 1, branches, raw, own)
    else:
        upper = ((me ^ round_mask) < me).astype(jnp.int32)
        part = lax.dynamic_index_in_dim(raw, 1 - upper, 0, keepdims=False)
        for bit in range(nblocks.bit_length() - 1):
            part = jnp.where(round_mask >> bit & 1 == 1, swap(part, "chan", 1 << bit), part)
        result = stacked(part, *own_lines(raw, upper), own)

    return result


def solution(mesh):
    in_specs = (
        P(("grp", "chan"), None, None, None),
        P(("grp", "chan"), None),
        P(),
        P(("grp", "chan")),
        P(("grp", "chan")),
    )
    out_specs = P(("grp", "chan"), None)
    return jax.shard_map(
        on_device, mesh=mesh, in_specs=in_specs, out_specs=out_specs, check_vma=False
    )
```

```python
import functools
import math

import jax
import jax.numpy as jnp
import numpy as np
from jax import lax
from jax.experimental import pallas as pl
from jax.experimental.pallas import tpu as pltpu
from jax.sharding import PartitionSpec as P

BAND = 128
LAGS = 1024
BINS_DEV = 8
PAIRS_DEV = 32


def self_pairs(nchan):
    return [(a, b) for a in range(nchan) for b in range(a + 1, nchan)]


def tables(nbands, nchan):
    nfreq = nbands * BAND
    half = nbands // 2
    nm = 2 * nbands
    nq = LAGS // nm
    square = nchan * nchan
    m = np.arange(nm)
    first = 2.0 * np.pi * ((m[:, None] * np.arange(nbands)[None, :]) % nm) / nm
    cos, sin = np.cos(first), np.sin(first)
    order = np.concatenate([np.arange(0, nq, 2), np.arange(1, nq, 2), np.full(nq // 2, nq)]) - nq // 2
    last = 2.0 * np.pi * ((order[:, None] * np.arange(BAND)[None, :]) % BAND) / BAND
    basis = np.zeros((2 * nm + 3 * nq // 2, 2 * BAND))
    for h in range(2):
        part = slice(h * half, (h + 1) * half)
        at = h * nbands
        basis[:nm, at : at + nbands] = np.concatenate([cos[:, part], -sin[:, part]], axis=1)
        basis[nm : 2 * nm, at : at + nbands] = np.concatenate([sin[:, part], cos[:, part]], axis=1)
    for line, (a, b) in enumerate(self_pairs(nchan)):
        basis[a * nchan + b, nm + line] = 1
        basis[b * nchan + a, nm + 2 * square + line] = 1
    for a in range(nchan):
        for b in range(nchan):
            line = square + a * nchan + b
            basis[line, nm + line] = 1
            basis[3 * square + b * nchan + a, nm + 2 * square + line] = 1
    lane = np.arange(1, BAND)
    basis[BAND - lane, BAND + lane] = 1
    basis[2 * nm :] = np.concatenate([np.cos(last), -np.sin(last)], axis=1)
    scale = 1.0 / math.sqrt(nfreq) / math.sqrt(PAIRS_DEV // BINS_DEV)
    angle = 2.0 * np.pi * (m[:, None] * np.arange(BAND)[None, :]) / (2 * nfreq)
    twiddle = np.stack([np.cos(angle), np.sin(angle)]) * scale
    return jnp.asarray(basis, jnp.bfloat16), jnp.asarray(twiddle, jnp.float32)


def prepare_kernel(
    raw_hbm, valid_hbm, partner_hbm, bins_hbm, count_hbm, raw_ref, own_ref, valid, partner, bins, count, sems
):
    nchan, nwin = valid.shape
    windows, rows = raw_hbm.shape[0], raw_ref.shape[2]
    moves = [(bins_hbm, bins), (count_hbm, count), (valid_hbm, valid), (partner_hbm, partner)]
    moves += [(raw_hbm.at[:, h * rows : (h + 1) * rows, :], raw_ref.at[h, 0:windows]) for h in range(2)]
    copies = [pltpu.make_async_copy(source, target, sems.at[k]) for k, (source, target) in enumerate(moves)]
    for copy in copies:
        copy.start()
    for copy in copies[:4]:
        copy.wait()
    number = lax.broadcasted_iota(jnp.int32, bins.shape, 1)
    kept = jnp.where(number < count[0], bins[...], -1)
    total = kept.shape[1]
    fill = jnp.zeros((1, BAND - total), jnp.int32)
    own_ref[...] = jnp.concatenate([partner[:, 0:1], fill[:, : total - 1], kept, fill[:, : BAND - 2 * total]], axis=1)
    row = lax.broadcasted_iota(jnp.int32, (rows, BAND), 0)
    notes = jnp.zeros((rows, BAND), jnp.int32)
    for place, values in ((0, kept >> 3), (1, kept & BINS_DEV - 1)):
        notes = jnp.where(row == place, jnp.concatenate([values, fill], axis=1), notes)
    for at in range(windows):
        c, w = at // nwin, at % nwin
        notes = jnp.where(row == rows - windows + at, valid[c, w], notes)
    for h in range(2):
        raw_ref[h, windows] = notes.astype(jnp.float32).astype(jnp.bfloat16)
    for copy in copies[4:]:
        copy.wait()


def bins_of(notes, count):
    digits = notes.astype(jnp.float32).astype(jnp.int32)
    return digits[0:1, 0:count] * BINS_DEV + digits[1:2, 0:count]


def valid_of(notes, windows, at):
    row = notes.shape[0] - windows + at
    return notes[row : row + 1, :]


def whiten(raw, valid, split):
    split[0 : raw.shape[0], :] = raw.astype(jnp.float32)
    bands = raw.shape[0] // 2
    real = split[pl.ds(0, bands, stride=2), :]
    imag = split[pl.ds(1, bands, stride=2), :]
    mean = jnp.sum(real * real + imag * imag, axis=-1, keepdims=True) * (1.0 / BAND)
    gain = lax.rsqrt(mean + 1e-06) * valid
    return [(part * gain).astype(jnp.bfloat16) for part in (real, imag)]


def cross_spectrum(left, right):
    real = imag = 0.0
    for (left_real, left_imag), (right_real, right_imag) in zip(left, right):
        real += left_real * right_real + left_imag * right_imag
        imag += left_imag * right_real - left_real * right_imag
    return [(part * (1.0 / len(left))).astype(jnp.bfloat16) for part in (real, imag)]


def lag_lines(table, spec, twiddle_ref, final, turned, numbers, lines, stride):
    nm = twiddle_ref.shape[1]
    cos, sin = twiddle_ref[0], twiddle_ref[1]
    out = jnp.dot(table, spec, preferred_element_type=jnp.float32)
    for at in range(len(numbers)):
        real = out[:nm, at * BAND : (at + 1) * BAND]
        imag = out[nm:, at * BAND : (at + 1) * BAND]
        turned[at * nm : (at + 1) * nm, 0:BAND] = (real * cos - imag * sin).astype(jnp.bfloat16)
        turned[at * nm : (at + 1) * nm, BAND : 2 * BAND] = (real * sin + imag * cos).astype(jnp.bfloat16)
    corr = lax.dot_general(final, turned[...], (((1,), (1,)), ((), ())), preferred_element_type=jnp.float32)
    nq = corr.shape[0] // 3
    low = lax.broadcasted_iota(jnp.int32, (nq, BAND), 1) < nm
    for at in range(0, len(numbers), 2):
        even, odd, beyond = (corr[k * nq : (k + 1) * nq, at * nm : (at + 2) * nm] for k in range(3))
        lines[pl.ds(numbers[at], nq, stride=stride), :] = jnp.where(low, even, pltpu.roll(odd, nm, 1))
        lines[pl.ds(numbers[at + 1], nq, stride=stride), :] = jnp.where(low, pltpu.roll(even, nm, 1), odd)
        for k in range(2):
            row = nq * stride + numbers[at + k]
            lines[row : row + 1, :] = (pltpu.roll(beyond, nm, 1) if k else beyond)[0:1, :]


def self_kernel(raw_ref, basis_ref, twiddle_ref, white_ref, lines_ref, split, spec, turned, *, nchan, nwin):
    half = white_ref.shape[2]
    lines_ref[...] = jnp.zeros(lines_ref.shape, jnp.float32)
    notes = raw_ref[0, nchan * nwin].astype(jnp.float32)
    for h in range(2):
        for at in range(nchan * nwin):
            valid = valid_of(notes, nchan * nwin, at)
            white = whiten(raw_ref[h, at], valid, split.at[h * nchan * nwin + at])
            for i in range(2):
                white_ref[h, 2 * at + i] = white[i]
        channels = [
            [[white_ref[h, 2 * (c * nwin + w) + i].astype(jnp.float32) for i in range(2)] for w in range(nwin)]
            for c in range(nchan)
        ]
        for at, (a, b) in enumerate(self_pairs(nchan)):
            real, imag = cross_spectrum(channels[a], channels[b])
            spec[2 * h * half : (2 * h + 1) * half, at * BAND : (at + 1) * BAND] = real
            spec[(2 * h + 1) * half : (2 * h + 2) * half, at * BAND : (at + 1) * BAND] = imag
    numbers = range(len(self_pairs(nchan)))
    nm = twiddle_ref.shape[1]
    lag_lines(
        basis_ref[0 : 2 * nm, 0:nm], spec[...], twiddle_ref, basis_ref[2 * nm :, :], turned, numbers, lines_ref, nchan * nchan
    )


def reversed_bits(value, bits):
    return sum((value >> k & 1) << bits - 1 - k for k in range(bits))


def stack_kernel(
    part_ref,
    white_ref,
    self_ref,
    own_ref,
    table_ref,
    basis_ref,
    twiddle_ref,
    keep_ref,
    send_ref,
    split,
    spec,
    turned,
    lines,
    *,
    nblocks,
    nchan,
    nwin,
):
    me = lax.axis_index("chan")
    half = white_ref.shape[1]
    square = nchan * nchan
    nq = lines.shape[0] // (2 * square) - 1
    nm = twiddle_ref.shape[1]
    for q in range(nq + 1):
        lines[q * 2 * square : q * 2 * square + square, :] = self_ref[q * square : (q + 1) * square, :]
        if q == nq:
            start = q * 2 * square + square
            lines[start : start + square, :] = jnp.zeros((square, BAND), jnp.float32)
    others = []
    notes = part_ref[nchan * nwin].astype(jnp.float32)
    for b in range(nchan):
        windows = [
            whiten(part_ref[at], valid_of(notes, nchan * nwin, at), split.at[at])
            for at in range(b * nwin, (b + 1) * nwin)
        ]
        others.append([[part.astype(jnp.float32) for part in parts] for parts in windows])
    for a in range(nchan):
        own = [[white_ref[2 * (a * nwin + w) + i].astype(jnp.float32) for i in range(2)] for w in range(nwin)]
        for b in range(nchan):
            real, imag = cross_spectrum(own, others[b])
            spec[a, 0:half, b * BAND : (b + 1) * BAND] = real
            spec[a, half : 2 * half, b * BAND : (b + 1) * BAND] = imag
    for a in range(nchan):
        numbers = [square + a * nchan + b for b in range(nchan)]
        lag_lines(
            table_ref[...], spec[a], twiddle_ref, basis_ref[2 * nm :, :], turned.at[a], numbers, lines, 2 * square
        )
    exact = [lines[q * 2 * square : (q + 1) * 2 * square, :] for q in range(nq + 1)]
    forward = [block.astype(jnp.bfloat16) for block in exact]
    negated = jnp.dot(
        jnp.concatenate([forward[nq - 1 - q] for q in range(nq)], axis=0),
        basis_ref[0:BAND, BAND : 2 * BAND],
        preferred_element_type=jnp.float32,
    )
    lane = lax.broadcasted_iota(jnp.int32, exact[0].shape, 1)
    backward = [
        jnp.where(lane == 0, exact[nq - q], negated[q * 2 * square : (q + 1) * 2 * square, :]).astype(jnp.bfloat16)
        for q in range(nq)
    ]
    both = jnp.concatenate([jnp.concatenate(parts, axis=1) for parts in (forward[:nq], backward)], axis=0)

    bits = nblocks.bit_length() - 1
    total = 2 * square
    bins = jnp.concatenate([own_ref[0:1, total : 2 * total], bins_of(part_ref[nchan * nwin], total)], axis=1)
    target = jnp.where(bins >= 0, bins ^ (me * BINS_DEV), -1)
    chunk = min(nblocks, 16)

    def add(index, _):
        place = lax.broadcasted_iota(jnp.int32, (chunk * BINS_DEV, 2 * total), 0) + index * chunk * BINS_DEV
        owned = (reversed_bits(place >> 3, bits) << 3) + (place & BINS_DEV - 1)
        chosen = (owned == target).astype(jnp.float32).astype(jnp.bfloat16)
        chosen = jnp.dot(chosen, basis_ref[0 : 2 * total, nm : 2 * nm], preferred_element_type=jnp.float32)
        sums = jnp.dot(chosen.astype(jnp.bfloat16), both, preferred_element_type=jnp.float32)

        def store(out_ref, blocks, first):
            for block in blocks:
                for q in range(0, nq, 2):
                    rows = slice(block * BINS_DEV, (block + 1) * BINS_DEV)
                    tile = jnp.concatenate([sums[rows, k * BAND : (k + 1) * BAND] for k in (q, q + 1)], axis=0)
                    start = ((first + block) * nq + q) * BINS_DEV
                    if not isinstance(start, int):
                        start = pl.multiple_of(start, 2 * BINS_DEV)
                    out_ref[pl.ds(start, 2 * BINS_DEV), :] = tile.astype(out_ref.dtype)

        if nblocks == chunk:
            store(send_ref, range(chunk // 2, chunk), -(chunk // 2))
            store(keep_ref, range(chunk // 2), 0)
        else:
            count = nblocks // 2 // chunk
            pl.when(index < count)(lambda: store(keep_ref, range(chunk), index * chunk))
            pl.when(index >= count)(lambda: store(send_ref, range(chunk), (index - count) * chunk))

    if nblocks == chunk:
        add(0, None)
    else:
        lax.fori_loop(0, nblocks // chunk, add, None)


def swap(values, axis, mask):
    return lax.ppermute(values, axis, [(p, p ^ mask) for p in range(lax.axis_size(axis))])


def on_device(spectra, valid, partner, pair_bin, pair_count):
    nblocks = lax.axis_size("chan")
    nchan, nwin, _, nfreq = spectra.shape
    nbands = nfreq // BAND
    half = nbands // 2
    nm = 2 * nbands
    nq = LAGS // nm // 2
    square = nchan * nchan
    windows = nchan * nwin
    npairs = len(self_pairs(nchan))
    me = lax.axis_index("chan")
    raw = spectra.reshape(windows, 2, nbands, BAND).transpose(0, 2, 1, 3).reshape(windows, 2 * nbands, BAND)
    basis, twiddle = tables(nbands, nchan)
    vmem = pl.BlockSpec(memory_space=pltpu.VMEM)
    hbm = pl.BlockSpec(memory_space=pltpu.HBM)
    params = pltpu.CompilerParams(vmem_limit_bytes=32 * 1024 * 1024)

    raw, own = pl.pallas_call(
        prepare_kernel,
        out_shape=[
            jax.ShapeDtypeStruct((2, windows + 1, nbands, BAND), jnp.bfloat16),
            jax.ShapeDtypeStruct((1, BAND), jnp.int32),
        ],
        in_specs=[hbm] * 5,
        out_specs=[vmem] * 2,
        scratch_shapes=[
            pltpu.SMEM(valid.shape, jnp.int32),
            pltpu.VMEM((1, nblocks), jnp.int32),
            pltpu.VMEM((1, pair_bin.shape[0]), jnp.int32),
            pltpu.SMEM((1,), jnp.int32),
            pltpu.SemaphoreType.DMA((6,)),
        ],
    )(raw, valid, partner.reshape(1, -1), pair_bin.reshape(1, -1), pair_count)

    def own_lines(raw, upper):
        white, lines = pl.pallas_call(
            functools.partial(self_kernel, nchan=nchan, nwin=nwin),
            out_shape=[
                jax.ShapeDtypeStruct((2, 2 * windows, half, BAND), jnp.bfloat16),
                jax.ShapeDtypeStruct(((nq + 1) * square, BAND), jnp.float32),
            ],
            in_specs=[vmem] * 3,
            out_specs=[vmem] * 2,
            scratch_shapes=[
                pltpu.VMEM((2 * windows, nbands + 8, BAND), jnp.float32),
                pltpu.VMEM((nm, npairs * BAND), jnp.bfloat16),
                pltpu.VMEM((npairs * nm, 2 * BAND), jnp.bfloat16),
            ],
            compiler_params=params,
        )(raw, basis, twiddle)
        table = lax.dynamic_slice(basis, (0, upper * nbands), (2 * nm, nbands))
        return lax.dynamic_index_in_dim(white, upper, 0, keepdims=False), lines, table

    def stacked(part, white, lines, table, own):
        rows = nblocks // 2 * BINS_DEV * nq
        keep, send = pl.pallas_call(
            functools.partial(stack_kernel, nblocks=nblocks, nchan=nchan, nwin=nwin),
            out_shape=[
                jax.ShapeDtypeStruct((rows, BAND), jnp.float32),
                jax.ShapeDtypeStruct((rows, BAND), jnp.bfloat16),
            ],
            in_specs=[vmem] * 7,
            out_specs=[vmem] * 2,
            scratch_shapes=[
                pltpu.VMEM((windows, nbands + 8, BAND), jnp.float32),
                pltpu.VMEM((nchan, nbands, nchan * BAND), jnp.bfloat16),
                pltpu.VMEM((nchan, nchan * nm, 2 * BAND), jnp.bfloat16),
                pltpu.VMEM(((nq + 1) * 2 * square, BAND), jnp.float32),
            ],
            compiler_params=params,
        )(part, white, lines, own, table, basis, twiddle)

        sums = keep + swap(send, "chan", 1).astype(jnp.float32)
        mask = 2
        while mask < nblocks:
            rows = sums.shape[0] // 2
            received = swap(sums[rows:].astype(jnp.bfloat16), "chan", mask)
            sums = sums[:rows] + received.astype(jnp.float32)
            mask *= 2
        return sums.reshape(nq, BINS_DEV, BAND).transpose(1, 0, 2).reshape(BINS_DEV, LAGS)

    def branch(mask, raw, own):
        upper = me >> mask.bit_length() - 1 & 1
        part = swap(lax.dynamic_index_in_dim(raw, 1 - upper, 0, keepdims=False), "chan", mask)
        return stacked(part, *own_lines(raw, upper), own)

    round_mask = own[0, 0]
    if nblocks <= 16:
        branches = [functools.partial(branch, mask) for mask in range(1, nblocks)]
        result = lax.switch(round_mask - 1, branches, raw, own)
    else:
        upper = ((me ^ round_mask) < me).astype(jnp.int32)
        part = lax.dynamic_index_in_dim(raw, 1 - upper, 0, keepdims=False)
        for bit in range(nblocks.bit_length() - 1):
            part = jnp.where(round_mask >> bit & 1 == 1, swap(part, "chan", 1 << bit), part)
        result = stacked(part, *own_lines(raw, upper), own)

    return result


def solution(mesh):
    in_specs = (
        P(("grp", "chan"), None, None, None),
        P(("grp", "chan"), None),
        P(),
        P(("grp", "chan")),
        P(("grp", "chan")),
    )
    out_specs = P(("grp", "chan"), None)
    return jax.shard_map(
        on_device, mesh=mesh, in_specs=in_specs, out_specs=out_specs, check_vma=False
    )
```
